32 devices in a mesh: day: 8 (over z, y), sta: 4 (over x, core).
Axes of the slice: x: 2, y: 2, z: 4, core: 2. Of those that a mesh axis runs over, the one named last changes fastest.
Arguments:
- spectra: bfloat16 [512, 2, 3, 96, 128], P('day', None, None, 'sta'), may hold values from -6 to 6
- src_block: int32 [2], replicated, may hold values from 0 to 3, as said below
- group_of: int32 [512], replicated, may hold values from 0 to 1, as said below
- owner: int32 [8], replicated, may hold values from 0 to 7, each once
Outputs:
- owned_stacks: float32 [8, 96, 2, 9, 128], P('day', 'sta')
The draws below stay inside these ranges and needn't reach their ends.
Inputs may be any that keep to these rules, and one draw needn't show every extreme that they name: `src_block`: the two entries differ. `group_of`: every one of the 2 groups has at least one segment. `owner`: each day index owns exactly one pair block.
All inputs are finite; a program needn't handle non-finite values.
Results may differ from the reference program's by a relative error of at most 0.0003.
Values may be sent and summed in bfloat16 or wider, within the bound.
No kernel may reach another device: no remote copies, remote signals or barrier semaphores. Data moves between devices by JAX's collectives and lax.ppermute only.
A program may use at most 64 MiB of HBM per device.

```python
import jax
import jax.numpy as jnp
from jax import lax

F = 128
LAG = 128
G = 2
SB = 4
R = 24
S = 8
STATIONS = 96
SEGS = 512
PB = 24
PAIRS = 96
N_DAY = 8
N_STA = 4


def draw_src_block(key, part):
    blocks = STATIONS // R
    other = jax.random.randint(jax.random.fold_in(key, 11), (), 0, blocks - 1)
    flipped = jax.random.randint(jax.random.fold_in(key, 12), (), 0, 2)
    last = jnp.int32(blocks - 1)
    first_entry = jnp.where(flipped == 1, other, last)
    second_entry = jnp.where(flipped == 1, last, other)
    return jnp.stack([first_entry, second_entry]).astype(jnp.int32)


def draw_group_of(key, part):
    drawn = jax.random.randint(jax.random.fold_in(key, 21), (SEGS,), 0, G)
    positions = jnp.arange(SEGS, dtype=jnp.int32)
    return jnp.where(positions < G, positions, drawn).astype(jnp.int32)


def levels(stream_key, extent, cuts, low, largest):
    def one(axis_at, parts):
        steps = jax.random.uniform(jax.random.fold_in(jax.random.fold_in(stream_key, 6), axis_at), (parts,), jnp.float32, low / len(cuts), largest / len(cuts))
        return jnp.repeat(jnp.exp(steps), extent[axis_at] // parts).reshape((-1,) + (1,) * (len(extent) - axis_at - 1))

    gain = one(*cuts[0])
    for cut in cuts[1:]:
        gain = gain * one(*cut)
    return gain


def centred(rng, dims, deviation, bound, split=(), kind=jnp.bfloat16):
    gain = levels(rng, dims, split, -0.22, 0.18) if split else 1.0
    values = jax.random.normal(rng, dims, jnp.float32) * deviation * gain
    return jnp.minimum(jnp.maximum(values, -bound), bound).astype(kind)


def setup_inputs(seed: int = 0) -> dict:
    key_list = jax.random.split(jax.random.key(seed), 5)
    return {
        "spectra": centred(key_list[0], (SEGS, 2, 3, STATIONS, F), 1.0, 6.0, ((0, 8), (3, 4))),
        "src_block": draw_src_block(jax.random.fold_in(key_list[4], 71), 0),
        "group_of": draw_group_of(jax.random.fold_in(key_list[4], 71), 0),
        "owner": jax.random.permutation(key_list[3], N_DAY).astype(jnp.int32),
    }


def lag_table(freqs, lags):
    freq_ids = jnp.arange(freqs, dtype=jnp.int32)
    lag_ids = jnp.arange(lags, dtype=jnp.int32) - lags // 2
    phase = jnp.mod(freq_ids[:, None] * lag_ids[None, :], 2 * freqs)
    angle = 2.0 * jnp.pi / (2 * freqs) * phase.astype(jnp.float32)
    weight = jnp.where(freq_ids == 0, 1.0, 2.0).astype(jnp.float32) / jnp.sqrt(jnp.float32(freqs))
    return jnp.concatenate([weight[:, None] * jnp.cos(angle), -weight[:, None] * jnp.sin(angle)], axis=0)

def reference(spectra, src_block, group_of, owner):
    station_ids = (src_block[:, None] * R + jnp.arange(SB, dtype=jnp.int32)[None, :]).reshape(-1).astype(jnp.int32)
    source_values = jnp.take(spectra, station_ids, axis=3).astype(jnp.float32)
    receiver_values = spectra.astype(jnp.float32)
    onehot = (group_of[None, :] == jnp.arange(G, dtype=jnp.int32)[:, None]).astype(jnp.float32)
    counts = lax.optimization_barrier(jnp.sum(onehot, axis=1))
    weighted = onehot[:, :, None, None, None, None] * source_values[None]
    real_part = jnp.einsum('gtpasf,tpbrf->srgabf', weighted, receiver_values)
    swapped = jnp.stack([receiver_values[:, 1], -receiver_values[:, 0]], axis=1)
    imag_part = jnp.einsum('gtpasf,tpbrf->srgabf', weighted, swapped)
    scale_rows = 1.0 / jnp.sqrt(counts)
    spectra_pairs = jnp.concatenate([real_part, imag_part], axis=-1) * scale_rows[None, None, :, None, None, None]
    table = lag_table(F, LAG)
    lagged = jnp.dot(spectra_pairs.reshape(-1, 2 * F), table, precision=lax.Precision.HIGHEST)
    lagged = lagged.reshape(S, N_STA, R, G, 9, LAG).transpose(1, 0, 2, 3, 4, 5)
    lagged = lagged.reshape(N_STA, N_DAY, PB, G, 9, LAG)
    day_ids = jnp.arange(N_DAY, dtype=jnp.int32)
    inverse = lax.optimization_barrier(jnp.sum(day_ids[None, :] * (owner[None, :] == day_ids[:, None]).astype(jnp.int32), axis=1)).astype(jnp.int32)
    ordered = jnp.take(lagged, inverse, axis=1).transpose(1, 0, 2, 3, 4, 5)
    return ordered.reshape(N_DAY, PAIRS, G, 9, LAG)
```

```python
import functools

import jax
import jax.numpy as jnp
import numpy as np
from jax import lax
from jax.experimental import pallas as pl
from jax.experimental.pallas import tpu as pltpu
from jax.sharding import PartitionSpec as P

F = 128
LAG = 128
G = 2
SB = 4
S = 8
COMPS = 3
XS = 2 * F + 8

f32 = jnp.float32
bf16 = jnp.bfloat16
PARAMS = pltpu.CompilerParams(vmem_limit_bytes=48 << 20)
VMEM = pl.BlockSpec(memory_space=pltpu.VMEM)
SMEM = pl.BlockSpec(memory_space=pltpu.SMEM)


def lag_table(freqs, lags):
    freq_ids = np.arange(freqs)
    lag_ids = np.arange(lags) - lags // 2
    angle = 2.0 * np.pi / (2 * freqs) * np.mod(freq_ids[:, None] * lag_ids[None, :], 2 * freqs)
    weight = np.where(freq_ids == 0, 1.0, 2.0)[:, None] / np.sqrt(freqs)
    table = np.concatenate([weight * np.cos(angle), -weight * np.sin(angle)], axis=0).astype(np.float32)
    high = table.astype(bf16)
    low = (table - high.astype(np.float32)).astype(bf16)
    return np.concatenate([high, low], axis=1)


def first_kernel(x_ref, o_ref, wide):
    rows = x_ref.shape[0] * 2
    for part in range(2):
        wide[part] = x_ref[:, part, 0].astype(f32)
    flat = wide.reshape(rows * 8, F)
    for s in range(SB):
        o_ref[0, s] = flat[pl.ds(s, rows, stride=8), :].T.astype(bf16)


def first_block(spectra):
    segs = spectra.shape[0]
    return pl.pallas_call(
        first_kernel,
        grid=(COMPS,),
        in_specs=[pl.BlockSpec((segs, 2, 1, 8, F), lambda b: (0, 0, b, 0, 0))],
        out_specs=pl.BlockSpec((1, SB, F, 2 * segs), lambda b: (b, 0, 0, 0)),
        out_shape=jax.ShapeDtypeStruct((COMPS, SB, F, 2 * segs), bf16),
        scratch_shapes=[pltpu.VMEM((2, segs, 8, F), f32)],
        compiler_params=PARAMS,
        name="first_block",
    )(spectra)


def receivers_kernel(x_ref, o_ref, wide, turned):
    b = pl.program_id(0)
    rows = x_ref.shape[0] * 2
    stations = x_ref.shape[3]
    for part in range(2):
        wide[part] = x_ref[:, part, 0].astype(f32)
    flat = wide.reshape(rows * stations, F)
    for r in range(stations):
        turned[pl.ds(b * stations + r, F, stride=COMPS * stations), :] = flat[pl.ds(r, rows, stride=stations), :].T

    @pl.when(b == COMPS - 1)
    def _():
        def body(f, carry):
            o_ref[f] = turned[pl.ds(pl.multiple_of(f * COMPS * stations, 8), COMPS * stations), :].astype(bf16)
            return carry

        lax.fori_loop(0, F, body, 0, unroll=8)


def receivers_by_freq(spectra):
    segs, stations = spectra.shape[0], spectra.shape[3]
    columns = COMPS * stations
    return pl.pallas_call(
        receivers_kernel,
        grid=(COMPS,),
        in_specs=[pl.BlockSpec((segs, 2, 1, stations, F), lambda b: (0, 0, b, 0, 0))],
        out_specs=pl.BlockSpec((F, columns, 2 * segs), lambda b: (0, 0, 0)),
        out_shape=jax.ShapeDtypeStruct((F, columns, 2 * segs), bf16),
        scratch_shapes=[pltpu.VMEM((2, segs, stations, F), f32), pltpu.VMEM((F * columns, 2 * segs), f32)],
        compiler_params=PARAMS,
        cost_estimate=pl.CostEstimate(flops=0, bytes_accessed=12 << 20, transcendentals=0),
        name="receivers_by_freq",
    )(spectra)


def stack_kernel(count, block_of, source_of, scale_ref, masks_ref, table_ref, recv_ref, *rest):
    blocks, (o_ref, src, cross) = rest[:-3], rest[-3:]
    columns = recv_ref.shape[1]
    half = recv_ref.shape[2] // 2
    rows = count * COMPS
    for d in range(count):
        which = block_of[source_of[d] // SB]
        station = source_of[d] % SB
        for j in range(len(blocks)):

            @pl.when(which == j)
            def _():
                for a in range(COMPS):
                    src[pl.ds(d * COMPS + a, F, stride=rows), :] = blocks[j][a, station].astype(f32)

    masks = masks_ref[...]

    def one_freq(f, carry):
        plain = src[pl.ds(f * rows, rows), :]
        rolled = pltpu.roll(plain, half, 1)
        left = [plain * masks[0:1], plain * masks[1:2], rolled * masks[2:3], rolled * masks[3:4]]
        left = jnp.concatenate(left, axis=0).astype(bf16)
        out = lax.dot_general(left, recv_ref[f], (((1,), (1,)), ((), ())), preferred_element_type=f32)
        cross[pl.ds(f, G * rows, stride=XS), 0:columns] = out[: G * rows]
        cross[pl.ds(F + f, G * rows, stride=XS), 0:columns] = out[G * rows :]
        return carry

    lax.fori_loop(0, F, one_freq, 0, unroll=4)
    table = table_ref[...]
    part = COMPS * columns
    for d in range(count):
        turned = []
        for g in range(G):
            for a in range(COMPS):
                first = (g * rows + d * COMPS + a) * XS
                turned.append(cross[first : first + 2 * F, :].T[:columns])
        turned = jnp.concatenate(turned, axis=0)
        high = turned.astype(bf16)
        low = (turned - high.astype(f32)).astype(bf16)
        both = jnp.dot(high, table, preferred_element_type=f32)
        lagged = both[:, :LAG] + both[:, LAG:] + jnp.dot(low, table[:, :LAG], preferred_element_type=f32)
        for g in range(G):
            o_ref[d, g * part : (g + 1) * part] = lagged[g * part : (g + 1) * part] * scale_ref[g]


def stacks(source_of, block_of, scale, masks, table, recv, blocks):
    count = source_of.shape[0]
    columns, depth = recv.shape[1:]
    rows = count * COMPS
    return pl.pallas_call(
        functools.partial(stack_kernel, count),
        in_specs=[SMEM, SMEM, SMEM, VMEM, VMEM, VMEM] + [VMEM] * len(blocks),
        out_specs=VMEM,
        out_shape=jax.ShapeDtypeStruct((count, G * COMPS * columns, LAG), f32),
        scratch_shapes=[pltpu.VMEM((F * rows, depth), f32), pltpu.VMEM((G * rows * XS, 128), f32)],
        compiler_params=PARAMS,
        cost_estimate=pl.CostEstimate(flops=0, bytes_accessed=16 << 20, transcendentals=0),
        name="stacks",
    )(block_of, source_of, scale, masks, table, recv, *blocks)


def total_kernel(stations, *refs):
    parts, o_ref = refs[:-1], refs[-1]
    per_station = G * COMPS * COMPS
    for g in range(G):
        for c in range(COMPS * COMPS):
            rows = pl.ds((g * COMPS * COMPS + c) * stations, stations)
            value = parts[0][rows, :]
            for part in parts[1:]:
                value = value + part[rows, :]
            o_ref[pl.ds(c * G + g, stations, stride=per_station), :] = value


def total(parts, stations):
    return pl.pallas_call(
        functools.partial(total_kernel, stations),
        in_specs=[VMEM] * len(parts),
        out_specs=VMEM,
        out_shape=jax.ShapeDtypeStruct(parts[0].shape, f32),
        compiler_params=PARAMS,
        name="total",
    )(*parts)


def swap(value, axis, mask):
    size = lax.axis_size(axis)
    return lax.ppermute(value, axis, [(i, i ^ mask) for i in range(size)])


def owned_block(owner):
    ids = jnp.arange(owner.shape[0], dtype=jnp.int32)
    return jnp.sum(ids[None, :] * (owner[None, :] == ids[:, None]).astype(jnp.int32), axis=1)


def local(spectra, src_block, group_of, owner):
    segs, stations = spectra.shape[0], spectra.shape[3]
    days = lax.axis_size("day")
    day = lax.axis_index("day")
    me = lax.axis_index("sta")
    group_ids = jnp.arange(G, dtype=jnp.int32)
    scale = 1.0 / jnp.sqrt(jnp.sum((group_of[None, :] == group_ids[:, None]).astype(f32), axis=1))
    mine = lax.dynamic_slice_in_dim(group_of, day * segs, segs)
    hot = (mine[None, :] == group_ids[:, None]).astype(f32)
    masks = jnp.concatenate([jnp.concatenate([hot, hot], axis=1), jnp.concatenate([-hot, hot], axis=1)], axis=0)
    table = jnp.asarray(lag_table(F, LAG))
    first = first_block(spectra)
    block_rows = S * stations // days

    if days == S and lax.axis_size("sta") == 4:
        across = swap(first, "sta", 2)
        blocks = [first, swap(first, "sta", 1), across, swap(across, "sta", 1)]
        recv = receivers_by_freq(spectra)
        owned = owned_block(owner)
        block_of = src_block ^ me
        z_masks = 2 * jnp.arange(days // 2, dtype=jnp.int32)
        away = stacks(jnp.take(owned, day ^ 1 ^ z_masks), block_of, scale, masks, table, recv, blocks)
        arrived = swap(away, "day", 1)
        kept = stacks(jnp.take(owned, day ^ z_masks), block_of, scale, masks, table, recv, blocks)
        kept = kept + arrived
        parts = [kept[0]] + [swap(kept[j], "day", 2 * j) for j in range(1, days // 2)]
        result = total(parts, stations)
        result = result.reshape(block_rows, COMPS * COMPS, G, LAG).transpose(0, 2, 1, 3)
        return result[None]

    gathered = lax.all_gather(first, "sta")
    blocks = [lax.dynamic_index_in_dim(gathered, src_block[k], 0, keepdims=False) for k in range(2)]
    recv = receivers_by_freq(spectra)
    every = jnp.arange(S, dtype=jnp.int32)
    partial = stacks(every, jnp.arange(2, dtype=jnp.int32), scale, masks, table, recv, blocks)
    partial = partial.reshape(S, G, COMPS * COMPS, stations, LAG).transpose(0, 3, 1, 2, 4)
    partial = partial.reshape(days, block_rows, G, COMPS * COMPS, LAG)
    ordered = jnp.take(partial, owned_block(owner), axis=0)
    return lax.psum_scatter(ordered, "day", scatter_dimension=0, tiled=True)


def solution(mesh):
    return jax.shard_map(
        local,
        mesh=mesh,
        in_specs=(P("day", None, None, "sta", None), P(), P(), P()),
        out_specs=P("day", "sta", None, None, None),
        check_vma=False,
    )
```

```python
import functools

import jax
import jax.numpy as jnp
import numpy as np
from jax import lax
from jax.experimental import pallas as pl
from jax.experimental.pallas import tpu as pltpu
from jax.sharding import PartitionSpec as P

F = 128
LAG = 128
G = 2
SB = 4
S = 8
COMPS = 3
XS = 2 * F + 8

f32 = jnp.float32
bf16 = jnp.bfloat16
f16 = jnp.float16
TOP = 14
PARAMS = pltpu.CompilerParams(vmem_limit_bytes=48 << 20)
VMEM = pl.BlockSpec(memory_space=pltpu.VMEM)
SMEM = pl.BlockSpec(memory_space=pltpu.SMEM)


def lag_table(freqs, lags):
    freq_ids = np.arange(freqs)
    lag_ids = np.arange(lags) - lags // 2
    angle = 2.0 * np.pi / (2 * freqs) * np.mod(freq_ids[:, None] * lag_ids[None, :], 2 * freqs)
    weight = np.where(freq_ids == 0, 1.0, 2.0)[:, None] / np.sqrt(freqs)
    table = np.concatenate([weight * np.cos(angle), -weight * np.sin(angle)], axis=0).astype(np.float32)
    high = table.astype(bf16)
    low = (table - high.astype(np.float32)).astype(bf16)
    return np.concatenate([high, low], axis=1)


def first_kernel(x_ref, o_ref, wide):
    rows = x_ref.shape[0] * 2
    for part in range(2):
        wide[part] = x_ref[:, part, 0].astype(f32)
    flat = wide.reshape(rows * 8, F)
    for s in range(SB):
        o_ref[0, s] = flat[pl.ds(s, rows, stride=8), :].T.astype(bf16)


def first_block(spectra):
    segs = spectra.shape[0]
    return pl.pallas_call(
        first_kernel,
        grid=(COMPS,),
        in_specs=[pl.BlockSpec((segs, 2, 1, 8, F), lambda b: (0, 0, b, 0, 0))],
        out_specs=pl.BlockSpec((1, SB, F, 2 * segs), lambda b: (b, 0, 0, 0)),
        out_shape=jax.ShapeDtypeStruct((COMPS, SB, F, 2 * segs), bf16),
        scratch_shapes=[pltpu.VMEM((2, segs, 8, F), f32)],
        compiler_params=PARAMS,
        name="first_block",
    )(spectra)


def receivers_kernel(x_ref, o_ref, wide, turned):
    b = pl.program_id(0)
    rows = x_ref.shape[0] * 2
    stations = x_ref.shape[3]
    for part in range(2):
        wide[part] = x_ref[:, part, 0].astype(f32)
    flat = wide.reshape(rows * stations, F)
    for r in range(stations):
        turned[pl.ds(b * stations + r, F, stride=COMPS * stations), :] = flat[pl.ds(r, rows, stride=stations), :].T

    @pl.when(b == COMPS - 1)
    def _():
        def body(f, carry):
            o_ref[f] = turned[pl.ds(pl.multiple_of(f * COMPS * stations, 8), COMPS * stations), :].astype(bf16)
            return carry

        lax.fori_loop(0, F, body, 0, unroll=8)


def receivers_by_freq(spectra):
    segs, stations = spectra.shape[0], spectra.shape[3]
    columns = COMPS * stations
    return pl.pallas_call(
        receivers_kernel,
        grid=(COMPS,),
        in_specs=[pl.BlockSpec((segs, 2, 1, stations, F), lambda b: (0, 0, b, 0, 0))],
        out_specs=pl.BlockSpec((F, columns, 2 * segs), lambda b: (0, 0, 0)),
        out_shape=jax.ShapeDtypeStruct((F, columns, 2 * segs), bf16),
        scratch_shapes=[pltpu.VMEM((2, segs, stations, F), f32), pltpu.VMEM((F * columns, 2 * segs), f32)],
        compiler_params=PARAMS,
        cost_estimate=pl.CostEstimate(flops=0, bytes_accessed=12 << 20, transcendentals=0),
        name="receivers_by_freq",
    )(spectra)


def power_of_two(n):
    size = jnp.abs(n)
    result = jnp.ones(n.shape, f32)
    for i in range(7):
        factor = jnp.where(n < 0, np.float32(2.0 ** -(2**i)), np.float32(2.0 ** (2**i)))
        result = result * jnp.where((size >> i) & 1 == 1, factor, np.float32(1.0))
    return result


def exponent_of(value):
    largest = jnp.max(jnp.abs(value), axis=(0, 1), keepdims=True)
    return jnp.ceil(jnp.log(jnp.maximum(largest, 1e-30)) * np.float32(1.4426950408889634)).astype(jnp.int32)


def stack_kernel(masks, coded, ids_ref, src_block_ref, owner_ref, scale_ref, masks_ref, table_ref, recv_ref, *rest):
    blocks, (o_ref, src, cross) = rest[:-3], rest[-3:]
    count = len(masks)
    columns = recv_ref.shape[1]
    half = recv_ref.shape[2] // 2
    rows = count * COMPS
    for d in range(count):
        dest = ids_ref[0] ^ masks[d]
        source = jnp.int32(0)
        for k in range(S):
            source = source + jnp.where(owner_ref[k] == dest, k, 0)
        which = ids_ref[1] ^ src_block_ref[source // SB]
        station = source % SB
        for j in range(len(blocks)):

            @pl.when(which == j)
            def _():
                for a in range(COMPS):
                    src[pl.ds(d * COMPS + a, F, stride=rows), :] = blocks[j][a, station].astype(f32)

    signs = masks_ref[...]

    def one_freq(f, carry):
        plain = src[pl.ds(f * rows, rows), :]
        rolled = pltpu.roll(plain, half, 1)
        left = [plain * signs[0:1], plain * signs[1:2], rolled * signs[2:3], rolled * signs[3:4]]
        left = jnp.concatenate(left, axis=0).astype(bf16)
        out = lax.dot_general(left, recv_ref[f], (((1,), (1,)), ((), ())), preferred_element_type=f32)
        cross[pl.ds(f, G * rows, stride=XS), 0:columns] = out[: G * rows]
        cross[pl.ds(F + f, G * rows, stride=XS), 0:columns] = out[G * rows :]
        return carry

    lax.fori_loop(0, F, one_freq, 0, unroll=32)
    table = table_ref[...]
    part = COMPS * columns
    exponents = jnp.zeros((16, LAG), f32)
    for d in range(count):
        turned = []
        for g in range(G):
            for a in range(COMPS):
                first = (g * rows + d * COMPS + a) * XS
                turned.append(cross[first : first + 2 * F, :].T[:columns])
        turned = jnp.concatenate(turned, axis=0)
        high = turned.astype(bf16)
        low = (turned - high.astype(f32)).astype(bf16)
        both = jnp.dot(high, table, preferred_element_type=f32)
        lagged = both[:, :LAG] + both[:, LAG:] + jnp.dot(low, table[:, :LAG], preferred_element_type=f32)
        lagged = jnp.concatenate([lagged[g * part : (g + 1) * part] * scale_ref[g] for g in range(G)], axis=0)
        if coded:
            e = exponent_of(lagged)
            lagged = lagged * power_of_two(TOP - e)
            exponents = jnp.where(lax.broadcasted_iota(jnp.int32, (16, LAG), 0) == d, e.astype(f32), exponents)
        o_ref[d * G * part : (d + 1) * G * part] = lagged
    if coded:
        o_ref[count * G * part :] = exponents


def stacks(masks, coded, ids, src_block, owner, scale, signs, table, recv, blocks):
    count = len(masks)
    columns, depth = recv.shape[1:]
    rows = count * COMPS
    out_rows = count * G * COMPS * columns + (16 if coded else 0)
    return pl.pallas_call(
        functools.partial(stack_kernel, masks, coded),
        in_specs=[SMEM] * 4 + [VMEM] * 3 + [VMEM] * len(blocks),
        out_specs=VMEM,
        out_shape=jax.ShapeDtypeStruct((out_rows, LAG), f32),
        scratch_shapes=[pltpu.VMEM((F * rows, depth), f32), pltpu.VMEM((G * rows * XS, 128), f32)],
        compiler_params=PARAMS,
        cost_estimate=pl.CostEstimate(flops=0, bytes_accessed=16 << 20, transcendentals=0),
        name="stacks",
    )(ids, src_block, owner, scale, signs, table, recv, *blocks)


def merge_kernel(kept_ref, arrived_ref, own_ref, *out_refs):
    size = own_ref.shape[0]
    count = len(out_refs) + 1
    tail = arrived_ref[count * size : count * size + 8]
    for j in range(count):
        back = power_of_two(tail[j : j + 1, 0:1].astype(jnp.int32) - TOP)
        rows = slice(j * size, (j + 1) * size)
        value = kept_ref[rows] + arrived_ref[rows] * back
        if j == 0:
            own_ref[...] = value
        else:
            e = exponent_of(value)
            out_refs[j - 1][0:size] = value * power_of_two(TOP - e)
            out_refs[j - 1][size:] = jnp.broadcast_to(e.astype(f32), (16, LAG))


def merge(kept, arrived, count):
    size = kept.shape[0] // count
    coded = jax.ShapeDtypeStruct((size + 16, LAG), f32)
    return pl.pallas_call(
        merge_kernel,
        in_specs=[VMEM] * 2,
        out_specs=[VMEM] * count,
        out_shape=[jax.ShapeDtypeStruct((size, LAG), f32)] + [coded] * (count - 1),
        compiler_params=PARAMS,
        name="merge",
    )(kept, arrived)


def total_kernel(stations, own_ref, *refs):
    parts, o_ref = refs[:-1], refs[-1]
    per_station = G * COMPS * COMPS
    size = own_ref.shape[0]
    back = [power_of_two(part[size : size + 1, 0:1].astype(jnp.int32) - TOP) for part in parts]
    for g in range(G):
        for c in range(COMPS * COMPS):
            rows = pl.ds((g * COMPS * COMPS + c) * stations, stations)
            value = own_ref[rows, :]
            for part, factor in zip(parts, back):
                value = value + part[rows, :] * factor
            o_ref[pl.ds(c * G + g, stations, stride=per_station), :] = value


def total(own, parts, stations):
    return pl.pallas_call(
        functools.partial(total_kernel, stations),
        in_specs=[VMEM] * (1 + len(parts)),
        out_specs=VMEM,
        out_shape=jax.ShapeDtypeStruct(own.shape, f32),
        compiler_params=PARAMS,
        name="total",
    )(own, *parts)


def swap(value, axis, mask):
    size = lax.axis_size(axis)
    return lax.ppermute(value, axis, [(i, i ^ mask) for i in range(size)])


def owned_block(owner):
    ids = jnp.arange(owner.shape[0], dtype=jnp.int32)
    return jnp.sum(ids[None, :] * (owner[None, :] == ids[:, None]).astype(jnp.int32), axis=1)


def local(spectra, src_block, group_of, owner):
    segs, stations = spectra.shape[0], spectra.shape[3]
    days = lax.axis_size("day")
    day = lax.axis_index("day")
    me = lax.axis_index("sta")
    group_ids = jnp.arange(G, dtype=jnp.int32)
    scale = 1.0 / jnp.sqrt(jnp.sum((group_of[None, :] == group_ids[:, None]).astype(f32), axis=1))
    mine = lax.dynamic_slice_in_dim(group_of, day * segs, segs)
    hot = (mine[None, :] == group_ids[:, None]).astype(f32)
    signs = jnp.concatenate([jnp.concatenate([hot, hot], axis=1), jnp.concatenate([-hot, hot], axis=1)], axis=0)
    table = jnp.asarray(lag_table(F, LAG))
    first = first_block(spectra)
    block_rows = S * stations // days

    if days == S and lax.axis_size("sta") == 4:
        across = swap(first, "sta", 2)
        blocks = [first, swap(first, "sta", 1), across, swap(across, "sta", 1)]
        recv = receivers_by_freq(spectra)
        ids = jnp.stack([day, me])
        masks = range(0, days, 2)
        operands = (ids, src_block, owner, scale, signs, table, recv, blocks)
        away = stacks([1 ^ mask for mask in masks], True, *operands)
        arrived = swap(away.astype(f16), "day", 1)
        kept = stacks(masks, False, *operands)
        own, *others = merge(kept, arrived.astype(f32), len(masks))
        parts = [swap(other.astype(f16), "day", mask).astype(f32) for other, mask in zip(others, masks[1:])]
        result = total(own, parts, stations)
        result = result.reshape(block_rows, COMPS * COMPS, G, LAG).transpose(0, 2, 1, 3)
        return result[None]

    gathered = lax.all_gather(first, "sta")
    blocks = [lax.dynamic_index_in_dim(gathered, src_block[k], 0, keepdims=False) for k in range(2)]
    recv = receivers_by_freq(spectra)
    every = jnp.arange(S, dtype=jnp.int32)
    partial = stacks(range(S), False, jnp.zeros(2, jnp.int32), every[:2], every, scale, signs, table, recv, blocks)
    partial = partial.reshape(S, G, COMPS * COMPS, stations, LAG).transpose(0, 3, 1, 2, 4)
    partial = partial.reshape(days, block_rows, G, COMPS * COMPS, LAG)
    ordered = jnp.take(partial, owned_block(owner), axis=0)
    return lax.psum_scatter(ordered, "day", scatter_dimension=0, tiled=True)


def solution(mesh):
    return jax.shard_map(
        local,
        mesh=mesh,
        in_specs=(P("day", None, None, "sta", None), P(), P(), P()),
        out_specs=P("day", "sta", None, None, None),
        check_vma=False,
    )
```

```python
import functools

import jax
import jax.numpy as jnp
import numpy as np
from jax import lax
from jax.experimental import pallas as pl
from jax.experimental.pallas import tpu as pltpu
from jax.sharding import PartitionSpec as P

F = 128
LAG = 128
G = 2
SB = 4
S = 8
COMPS = 3
XS = 2 * F + 8

f32 = jnp.float32
bf16 = jnp.bfloat16
f16 = jnp.float16
TOP = 14
PARAMS = pltpu.CompilerParams(vmem_limit_bytes=48 << 20)
VMEM = pl.BlockSpec(memory_space=pltpu.VMEM)
SMEM = pl.BlockSpec(memory_space=pltpu.SMEM)


def lag_table(freqs, lags):
    freq_ids = np.arange(freqs)
    lag_ids = np.arange(lags) - lags // 2
    angle = 2.0 * np.pi / (2 * freqs) * np.mod(freq_ids[:, None] * lag_ids[None, :], 2 * freqs)
    weight = np.where(freq_ids == 0, 1.0, 2.0)[:, None] / np.sqrt(freqs)
    return np.concatenate([weight * np.cos(angle), -weight * np.sin(angle)], axis=0).astype(np.float32)


def two_terms(value):
    high = value.astype(bf16)
    return high, (value - high.astype(f32)).astype(bf16)


def first_kernel(x_hbm, o_ref, near, wide, sem):
    rows = near.shape[1] * 2
    copies = [
        pltpu.make_async_copy(x_hbm.at[:, :, a, 0:8, :], near.at[a], sem.at[a]) for a in range(COMPS)
    ]
    for copy in copies:
        copy.start()
    for a in range(COMPS):
        copies[a].wait()
        for part in range(2):
            wide[a, part] = near[a, :, part].astype(f32)
        flat = wide.at[a].reshape(rows * 8, F)
        for s in range(SB):
            o_ref[a, s] = flat[pl.ds(s, rows, stride=8), :].T.astype(bf16)


def first_block(spectra):
    segs = spectra.shape[0]
    return pl.pallas_call(
        first_kernel,
        in_specs=[pl.BlockSpec(memory_space=pltpu.HBM)],
        out_specs=VMEM,
        out_shape=jax.ShapeDtypeStruct((COMPS, SB, F, 2 * segs), bf16),
        scratch_shapes=[
            pltpu.VMEM((COMPS, segs, 2, 8, F), bf16),
            pltpu.VMEM((COMPS, 2, segs, 8, F), f32),
            pltpu.SemaphoreType.DMA((COMPS,)),
        ],
        compiler_params=PARAMS,
        name="first_block",
    )(spectra)


def receivers_kernel(x_ref, o_ref, wide, turned):
    b = pl.program_id(0)
    rows = x_ref.shape[0] * 2
    stations = x_ref.shape[3]
    for part in range(2):
        wide[part] = x_ref[:, part, 0].astype(f32)
    flat = wide.reshape(rows * stations, F)
    for r in range(stations):
        turned[pl.ds(b * stations + r, F, stride=COMPS * stations), :] = flat[pl.ds(r, rows, stride=stations), :].T

    @pl.when(b == COMPS - 1)
    def _():
        def body(f, carry):
            o_ref[f] = turned[pl.ds(pl.multiple_of(f * COMPS * stations, 8), COMPS * stations), :].astype(bf16)
            return carry

        lax.fori_loop(0, F, body, 0, unroll=8)


def receivers_by_freq(spectra):
    segs, stations = spectra.shape[0], spectra.shape[3]
    columns = COMPS * stations
    return pl.pallas_call(
        receivers_kernel,
        grid=(COMPS,),
        in_specs=[pl.BlockSpec((segs, 2, 1, stations, F), lambda b: (0, 0, b, 0, 0))],
        out_specs=pl.BlockSpec((F, columns, 2 * segs), lambda b: (0, 0, 0)),
        out_shape=jax.ShapeDtypeStruct((F, columns, 2 * segs), bf16),
        scratch_shapes=[pltpu.VMEM((2, segs, stations, F), f32), pltpu.VMEM((F * columns, 2 * segs), f32)],
        compiler_params=PARAMS,
        cost_estimate=pl.CostEstimate(flops=0, bytes_accessed=12 << 20, transcendentals=0),
        name="receivers_by_freq",
    )(spectra)


def power_of_two(n):
    size = jnp.abs(n)
    result = jnp.ones(n.shape, f32)
    for i in range(7):
        factor = jnp.where(n < 0, np.float32(2.0 ** -(2**i)), np.float32(2.0 ** (2**i)))
        result = result * jnp.where((size >> i) & 1 == 1, factor, np.float32(1.0))
    return result


def exponent_of(value):
    largest = jnp.max(jnp.abs(value), axis=(0, 1), keepdims=True)
    return jnp.ceil(jnp.log(jnp.maximum(largest, 1e-30)) * np.float32(1.4426950408889634)).astype(jnp.int32)


def pairs_of(outputs):
    pairs = [(mask, a) for _, blocks in outputs for mask, comps in blocks for a in comps]
    return pairs, -(-len(pairs) // 8) * 8


def stack_kernel(outputs, ids_ref, src_block_ref, owner_ref, scale_ref, signs_ref, table_ref, recv_ref, *rest):
    blocks, o_refs, (src, cross) = rest[: -2 - len(outputs)], rest[-2 - len(outputs) : -2], rest[-2:]
    pairs, rows = pairs_of(outputs)
    columns = recv_ref.shape[1]
    half = recv_ref.shape[2] // 2
    for mask in sorted({mask for mask, _ in pairs}):
        dest = ids_ref[0] ^ mask
        source = jnp.int32(0)
        for k in range(S):
            source = source + jnp.where(owner_ref[k] == dest, k, 0)
        which = ids_ref[1] ^ src_block_ref[source // SB]
        station = source % SB
        for j in range(len(blocks)):

            @pl.when(which == j)
            def _():
                for at, (pair_mask, a) in enumerate(pairs):
                    if pair_mask == mask:
                        src[pl.ds(at, F, stride=rows), :] = blocks[j][a, station].astype(f32)

    signs = signs_ref[...]

    def one_freq(f, carry):
        plain = src[pl.ds(pl.multiple_of(f * rows, 8), rows), :]
        rolled = pltpu.roll(plain, half, 1)
        left = [plain * signs[0:1], plain * signs[1:2], rolled * signs[2:3], rolled * signs[3:4]]
        left = jnp.concatenate(left, axis=0).astype(bf16)
        out = lax.dot_general(left, recv_ref[f], (((1,), (1,)), ((), ())), preferred_element_type=f32)
        cross[pl.ds(f, G * rows, stride=XS), 0:columns] = out[: G * rows]
        cross[pl.ds(F + f, G * rows, stride=XS), 0:columns] = out[G * rows :]
        return carry

    lax.fori_loop(0, F, one_freq, 0, unroll=32)
    table_high, table_low = two_terms(table_ref[...])
    table = jnp.concatenate([table_high, table_low], axis=1)
    for (coded, blocks_of), o_ref in zip(outputs, o_refs):
        exponents = jnp.zeros((16, LAG), f32)
        done = 0
        for at, (mask, comps) in enumerate(blocks_of):
            turned = []
            for g in range(G):
                for a in comps:
                    first = (g * rows + pairs.index((mask, a))) * XS
                    turned.append(cross[first : first + 2 * F, :].T[:columns])
            high, low = two_terms(jnp.concatenate(turned, axis=0))
            both = jnp.dot(high, table, preferred_element_type=f32)
            lagged = both[:, :LAG] + both[:, LAG:] + jnp.dot(low, table_high, preferred_element_type=f32)
            part = len(comps) * columns
            lagged = jnp.concatenate([lagged[g * part : (g + 1) * part] * scale_ref[g] for g in range(G)], axis=0)
            if coded:
                e = exponent_of(lagged)
                lagged = lagged * power_of_two(TOP - e)
                exponents = jnp.where(lax.broadcasted_iota(jnp.int32, (16, LAG), 0) == at, e.astype(f32), exponents)
            o_ref[done : done + G * part] = lagged
            done += G * part
        if coded:
            o_ref[done:] = exponents


def stacks(outputs, ids, src_block, owner, scale, signs, table, recv, blocks):
    columns, depth = recv.shape[1:]
    rows = pairs_of(outputs)[1]
    shapes = []
    for coded, blocks_of in outputs:
        size = sum(G * len(comps) * columns for _, comps in blocks_of) + (16 if coded else 0)
        shapes.append(jax.ShapeDtypeStruct((size, LAG), f32))
    return pl.pallas_call(
        functools.partial(stack_kernel, outputs),
        in_specs=[SMEM] * 4 + [VMEM] * 3 + [VMEM] * len(blocks),
        out_specs=[VMEM] * len(outputs),
        out_shape=shapes,
        scratch_shapes=[pltpu.VMEM((F * rows, depth), f32), pltpu.VMEM((G * rows * XS, 128), f32)],
        compiler_params=PARAMS,
        cost_estimate=pl.CostEstimate(flops=0, bytes_accessed=16 << 20, transcendentals=0),
        name="stacks",
    )(ids, src_block, owner, scale, signs, table, recv, *blocks)


def factor_of(coded, size, at):
    return power_of_two(coded[size + at : size + at + 1, 0:1].astype(jnp.int32) - TOP)


def store_coded(o_ref, value):
    size = value.shape[0]
    e = exponent_of(value)
    o_ref[0:size] = value * power_of_two(TOP - e)
    o_ref[size:] = jnp.broadcast_to(e.astype(f32), (16, LAG))


def merge_kernel(count, kept_ref, *refs):
    size = kept_ref.shape[0] // count
    arrived, own_ref, out_refs = refs[:-count], refs[-count], refs[len(refs) - count + 1 :]
    factors = [[factor_of(ref, count * size, j) for j in range(count)] for ref in arrived]
    for j in range(count):
        rows = slice(j * size, (j + 1) * size)
        value = kept_ref[rows]
        for ref, factor in zip(arrived, factors):
            value = value + ref[rows] * factor[j]
        if j == 0:
            own_ref[...] = value
        else:
            store_coded(out_refs[j - 1], value)


def merge(kept, arrived, count):
    size = kept.shape[0] // count
    coded = jax.ShapeDtypeStruct((size + 16, LAG), f32)
    return pl.pallas_call(
        functools.partial(merge_kernel, count),
        in_specs=[VMEM] * (1 + len(arrived)),
        out_specs=[VMEM] * count,
        out_shape=[jax.ShapeDtypeStruct((size, LAG), f32)] + [coded] * (count - 1),
        compiler_params=PARAMS,
        name="merge",
    )(kept, *arrived)


def total_kernel(stations, comps, counts, *refs):
    refs, o_ref = list(refs[:-1]), refs[-1]
    per_station = G * COMPS * COMPS
    for of, count in zip(comps, counts):
        own_ref, parts, refs = refs[0], refs[1:count], refs[count:]
        size = own_ref.shape[0]
        factors = [factor_of(part, size, 0) for part in parts]
        at = 0
        for g in range(G):
            for a in of:
                for b in range(COMPS):
                    rows = pl.ds(at, stations)
                    at += stations
                    value = own_ref[rows, :]
                    for part, factor in zip(parts, factors):
                        value = value + part[rows, :] * factor
                    o_ref[pl.ds((a * COMPS + b) * G + g, stations, stride=per_station), :] = value


def total(stations, comps, parts):
    counts = [len(of) for of in parts]
    return pl.pallas_call(
        functools.partial(total_kernel, stations, comps, counts),
        in_specs=[VMEM] * sum(counts),
        out_specs=VMEM,
        out_shape=jax.ShapeDtypeStruct((stations * COMPS * COMPS * G, LAG), f32),
        compiler_params=PARAMS,
        name="total",
    )(*[part for of in parts for part in of])


def swap(value, axis, mask):
    size = lax.axis_size(axis)
    return lax.ppermute(value, axis, [(i, i ^ mask) for i in range(size)])


def send(coded, mask):
    return swap(coded.astype(f16), "day", mask).astype(f32)


def owned_block(owner):
    ids = jnp.arange(owner.shape[0], dtype=jnp.int32)
    return jnp.sum(ids[None, :] * (owner[None, :] == ids[:, None]).astype(jnp.int32), axis=1)


def local(spectra, src_block, group_of, owner):
    segs, stations = spectra.shape[0], spectra.shape[3]
    days = lax.axis_size("day")
    day = lax.axis_index("day")
    me = lax.axis_index("sta")
    group_ids = jnp.arange(G, dtype=jnp.int32)
    scale = 1.0 / jnp.sqrt(jnp.sum((group_of[None, :] == group_ids[:, None]).astype(f32), axis=1))
    mine = lax.dynamic_slice_in_dim(group_of, day * segs, segs)
    hot = (mine[None, :] == group_ids[:, None]).astype(f32)
    signs = jnp.concatenate([jnp.concatenate([hot, hot], axis=1), jnp.concatenate([-hot, hot], axis=1)], axis=0)
    table = jnp.asarray(lag_table(F, LAG))
    first = first_block(spectra)
    block_rows = S * stations // days

    if days == S and lax.axis_size("sta") == 4:
        across = swap(first, "sta", 2)
        blocks = [first, swap(first, "sta", 1), across, swap(across, "sta", 1)]
        recv = receivers_by_freq(spectra)
        operands = (jnp.stack([day, me]), src_block, owner, scale, signs, table, recv, blocks)
        ys, zs = [0, 1], range(0, days, 2)
        y_first, z_first = (0, 1), (2,)
        away = stacks(
            [(True, [(1 ^ z, y_first) for z in zs])]
            + [(True, [(y ^ z, z_first) for y in ys]) for z in zs[1:]],
            *operands,
        )
        arrived_y = send(away[0], 1)
        arrived_z = [send(part, z) for part, z in zip(away[1:], zs[1:])]
        kept = stacks([(False, [(z, y_first) for z in zs]), (False, [(y, z_first) for y in ys])], *operands)
        own_y, *others = merge(kept[0], [arrived_y], len(zs))
        parts_y = [own_y] + [send(other, z) for other, z in zip(others, zs[1:])]
        own_z, other = merge(kept[1], arrived_z, len(ys))
        result = total(stations, (y_first, z_first), (parts_y, [own_z, send(other, 1)]))
        result = result.reshape(block_rows, COMPS * COMPS, G, LAG).transpose(0, 2, 1, 3)
        return result[None]

    gathered = lax.all_gather(first, "sta")
    blocks = [lax.dynamic_index_in_dim(gathered, src_block[k], 0, keepdims=False) for k in range(2)]
    recv = receivers_by_freq(spectra)
    every = jnp.arange(S, dtype=jnp.int32)
    outputs = [(False, [(mask, tuple(range(COMPS))) for mask in range(S)])]
    (partial,) = stacks(outputs, jnp.zeros(2, jnp.int32), every[:2], every, scale, signs, table, recv, blocks)
    partial = partial.reshape(S, G, COMPS * COMPS, stations, LAG).transpose(0, 3, 1, 2, 4)
    partial = partial.reshape(days, block_rows, G, COMPS * COMPS, LAG)
    ordered = jnp.take(partial, owned_block(owner), axis=0)
    return lax.psum_scatter(ordered, "day", scatter_dimension=0, tiled=True)


def solution(mesh):
    return jax.shard_map(
        local,
        mesh=mesh,
        in_specs=(P("day", None, None, "sta", None), P(), P(), P()),
        out_specs=P("day", "sta", None, None, None),
        check_vma=False,
    )
```

```python
import functools

import jax
import jax.numpy as jnp
import numpy as np
from jax import lax
from jax.experimental import pallas as pl
from jax.experimental.pallas import tpu as pltpu
from jax.sharding import PartitionSpec as P

F = 128
LAG = 128
G = 2
SB = 4
S = 8
COMPS = 3
XS = 2 * F + 8

f32 = jnp.float32
bf16 = jnp.bfloat16
f16 = jnp.float16
TAIL = 8
TOP = 14
PARAMS = pltpu.CompilerParams(vmem_limit_bytes=24 << 20)
VMEM = pl.BlockSpec(memory_space=pltpu.VMEM)
SMEM = pl.BlockSpec(memory_space=pltpu.SMEM)


def lag_table(freqs, lags):
    freq_ids = np.arange(freqs)
    lag_ids = np.arange(lags) - lags // 2
    angle = 2.0 * np.pi / (2 * freqs) * np.mod(freq_ids[:, None] * lag_ids[None, :], 2 * freqs)
    weight = np.where(freq_ids == 0, 1.0, 2.0)[:, None] / np.sqrt(freqs)
    return np.concatenate([weight * np.cos(angle), -weight * np.sin(angle)], axis=0).astype(np.float32)


def two_terms(value):
    high = value.astype(bf16)
    return high, (value - high.astype(f32)).astype(bf16)


def first_kernel(shares, x_ref, *refs):
    o_refs, wide = refs[:-1], refs[-1]
    rows = x_ref.shape[0] * 2
    for a in range(COMPS):
        for part in range(2):
            wide[a, part] = x_ref[:, part, a, 0:8].astype(f32)
        flat = wide.at[a].reshape(rows * 8, F)
        for of, o_ref in zip(shares, o_refs):
            if a in of:
                for s in range(SB):
                    o_ref[of.index(a), s] = flat[pl.ds(s, rows, stride=8), :].T.astype(bf16)


def first_block(spectra, shares):
    segs = spectra.shape[0]
    return pl.pallas_call(
        functools.partial(first_kernel, shares),
        in_specs=[VMEM],
        out_specs=[VMEM] * len(shares),
        out_shape=[jax.ShapeDtypeStruct((len(of), SB, F, 2 * segs), bf16) for of in shares],
        scratch_shapes=[pltpu.VMEM((COMPS, 2, segs, 8, F), f32)],
        compiler_params=PARAMS,
        name="first_block",
    )(spectra)


def receivers_kernel(ids_ref, x_ref, group_ref, o_ref, signs_ref, scale_ref, wide, turned):
    b = pl.program_id(0)
    rows = x_ref.shape[0] * 2
    stations = x_ref.shape[3]
    for part in range(2):
        wide[part] = x_ref[:, part, 0].astype(f32)
    flat = wide.reshape(rows * stations, F)
    for r in range(stations):
        turned[pl.ds(b * stations + r, F, stride=COMPS * stations), :] = flat[pl.ds(r, rows, stride=stations), :].T

    @pl.when(b == 0)
    def _():
        at = ids_ref[0] * (rows // 2)
        row = group_ref[pl.ds(at // rows, 1), :].astype(f32)
        swapped = pltpu.roll(row, rows // 2, 1)
        low = lax.broadcasted_iota(jnp.int32, row.shape, 1) < rows // 2
        mine = jnp.where(low == (at % rows == 0), row, swapped)
        for g in range(G):
            hot = jnp.where(mine == g, np.float32(1.0), np.float32(0.0))
            signs_ref[g : g + 1] = hot
            signs_ref[G + g : G + g + 1] = jnp.where(low, -hot, hot)
            hits = jnp.where(group_ref[...] == g, np.float32(1.0), np.float32(0.0))
            count = jnp.sum(hits, axis=(0, 1), keepdims=True)
            scale_ref[g : g + 1] = jnp.broadcast_to(1.0 / jnp.sqrt(count), (1, LAG))

    @pl.when(b == COMPS - 1)
    def _():
        def body(f, carry):
            o_ref[f] = turned[pl.ds(pl.multiple_of(f * COMPS * stations, 8), COMPS * stations), :].astype(bf16)
            return carry

        lax.fori_loop(0, F, body, 0, unroll=8)


def receivers_by_freq(ids, spectra, group_of):
    segs, stations = spectra.shape[0], spectra.shape[3]
    columns = COMPS * stations
    groups = group_of.reshape(-1, 2 * segs)
    fixed = lambda b: (0, 0)
    return pl.pallas_call(
        receivers_kernel,
        grid=(COMPS,),
        in_specs=[
            SMEM,
            pl.BlockSpec((segs, 2, 1, stations, F), lambda b: (0, 0, b, 0, 0)),
            pl.BlockSpec(groups.shape, fixed),
        ],
        out_specs=[
            pl.BlockSpec((F, columns, 2 * segs), lambda b: (0, 0, 0)),
            pl.BlockSpec((2 * G, 2 * segs), fixed),
            pl.BlockSpec((G, LAG), fixed),
        ],
        out_shape=[
            jax.ShapeDtypeStruct((F, columns, 2 * segs), bf16),
            jax.ShapeDtypeStruct((2 * G, 2 * segs), f32),
            jax.ShapeDtypeStruct((G, LAG), f32),
        ],
        scratch_shapes=[pltpu.VMEM((2, segs, stations, F), f32), pltpu.VMEM((F * columns, 2 * segs), f32)],
        compiler_params=PARAMS,
        cost_estimate=pl.CostEstimate(flops=0, bytes_accessed=12 << 20, transcendentals=0),
        name="receivers_by_freq",
    )(ids, spectra, groups)


def power_of_two(n):
    size = jnp.abs(n)
    result = jnp.ones(n.shape, f32)
    for i in range(7):
        factor = jnp.where(n < 0, np.float32(2.0 ** -(2**i)), np.float32(2.0 ** (2**i)))
        result = result * jnp.where((size >> i) & 1 == 1, factor, np.float32(1.0))
    return result


def exponent_of(value):
    largest = jnp.max(jnp.abs(value), axis=(0, 1), keepdims=True)
    return jnp.ceil(jnp.log(jnp.maximum(largest, 1e-30)) * np.float32(1.4426950408889634)).astype(jnp.int32)


def rows_of(pairs):
    return -(-len(pairs) // 8) * 8


def cross_kernel(pairs, comps_of, ids_ref, src_block_ref, owner_ref, recv_ref, signs_ref, *rest):
    blocks, (o_ref, src) = rest[:-2], rest[-2:]
    rows = rows_of(pairs)
    columns = recv_ref.shape[1]
    half = recv_ref.shape[2] // 2
    for mask in sorted({mask for mask, _ in pairs}):
        dest = ids_ref[0] ^ mask
        source = jnp.int32(0)
        for k in range(S):
            source = source + jnp.where(owner_ref[k] == dest, k, 0)
        which = ids_ref[1] ^ src_block_ref[source // SB]
        station = source % SB
        for j in range(len(blocks)):

            @pl.when(which == j)
            def _():
                for at, (pair_mask, a) in enumerate(pairs):
                    if pair_mask == mask:
                        src[pl.ds(at, F, stride=rows), :] = blocks[j][comps_of.index(a), station].astype(f32)

    signs = signs_ref[...]

    def one_freq(f, carry):
        plain = src[pl.ds(pl.multiple_of(f * rows, 8), rows), :]
        rolled = pltpu.roll(plain, half, 1)
        left = [plain * signs[0:1], plain * signs[1:2], rolled * signs[2:3], rolled * signs[3:4]]
        left = jnp.concatenate(left, axis=0).astype(bf16)
        out = lax.dot_general(left, recv_ref[f], (((1,), (1,)), ((), ())), preferred_element_type=f32)
        o_ref[pl.ds(f, G * rows, stride=XS), 0:columns] = out[: G * rows]
        o_ref[pl.ds(F + f, G * rows, stride=XS), 0:columns] = out[G * rows :]
        return carry

    lax.fori_loop(0, F, one_freq, 0, unroll=F)


def cross_spectra(pairs, comps_of, ids, src_block, owner, recv, signs, blocks):
    depth = recv.shape[2]
    rows = rows_of(pairs)
    return pl.pallas_call(
        functools.partial(cross_kernel, pairs, comps_of),
        in_specs=[SMEM] * 3 + [VMEM] * (2 + len(blocks)),
        out_specs=VMEM,
        out_shape=jax.ShapeDtypeStruct((G * rows * XS, 128), f32),
        scratch_shapes=[pltpu.VMEM((F * rows, depth), f32)],
        compiler_params=PARAMS,
        cost_estimate=pl.CostEstimate(flops=0, bytes_accessed=10 << 20, transcendentals=0),
        name="cross_spectra",
    )(ids, src_block, owner, recv, signs, *blocks)


def lag_kernel(outputs, pairs, columns, cross_ref, table_ref, scale_ref, *o_refs):
    rows = rows_of(pairs)
    table_high, table_low = two_terms(table_ref[...])
    table = jnp.concatenate([table_high, table_low], axis=1)
    for (coded, blocks_of), o_ref in zip(outputs, o_refs):
        exponents = jnp.zeros((TAIL, LAG), f32)
        done = 0
        for at, (mask, comps) in enumerate(blocks_of):
            turned = []
            for g in range(G):
                for a in comps:
                    first = (g * rows + pairs.index((mask, a))) * XS
                    turned.append(cross_ref[first : first + 2 * F, :].T[:columns])
            high, low = two_terms(jnp.concatenate(turned, axis=0))
            both = jnp.dot(high, table, preferred_element_type=f32)
            lagged = both[:, :LAG] + both[:, LAG:] + jnp.dot(low, table_high, preferred_element_type=f32)
            part = len(comps) * columns
            lagged = [lagged[g * part : (g + 1) * part] * scale_ref[g : g + 1] for g in range(G)]
            lagged = jnp.concatenate(lagged, axis=0)
            if coded:
                e = exponent_of(lagged)
                lagged = lagged * power_of_two(TOP - e)
                exponents = jnp.where(lax.broadcasted_iota(jnp.int32, (TAIL, LAG), 0) == at, e.astype(f32), exponents)
            o_ref[done : done + G * part] = lagged
            done += G * part
        if coded:
            o_ref[done:] = exponents


def lag_transform(outputs, pairs, columns, cross, table, scale):
    shapes = []
    for coded, blocks_of in outputs:
        size = sum(G * len(comps) * columns for _, comps in blocks_of) + (TAIL if coded else 0)
        shapes.append(jax.ShapeDtypeStruct((size, LAG), f32))
    return pl.pallas_call(
        functools.partial(lag_kernel, outputs, pairs, columns),
        in_specs=[VMEM] * 3,
        out_specs=[VMEM] * len(outputs),
        out_shape=shapes,
        compiler_params=PARAMS,
        cost_estimate=pl.CostEstimate(flops=0, bytes_accessed=5 << 20, transcendentals=0),
        name="lag_transform",
    )(cross, table, scale)


def factor_of(coded, size, at):
    return power_of_two(coded[size + at : size + at + 1, 0:1].astype(jnp.int32) - TOP)


def store_coded(o_ref, value):
    size = value.shape[0]
    e = exponent_of(value)
    o_ref[0:size] = value * power_of_two(TOP - e)
    o_ref[size:] = jnp.broadcast_to(e.astype(f32), (TAIL, LAG))


def merge_kernel(count, first, kept_ref, *refs):
    size = kept_ref.shape[0] // count
    arrived, o_refs = refs[:-count], refs[-count:]
    factors = [[factor_of(ref, count * size, j) for j in range(count)] for ref in arrived]
    for j in range(count):
        rows = slice(j * size, (j + 1) * size)
        value = kept_ref[rows]
        for ref, factor in zip(arrived, factors):
            value = value + ref[rows] * factor[j]
        if j < first:
            o_refs[j][...] = value
        else:
            store_coded(o_refs[j], value)


def merge(kept, arrived, count, first):
    size = kept.shape[0] // count
    plain, coded = jax.ShapeDtypeStruct((size, LAG), f32), jax.ShapeDtypeStruct((size + TAIL, LAG), f32)
    return pl.pallas_call(
        functools.partial(merge_kernel, count, first),
        in_specs=[VMEM] * (1 + len(arrived)),
        out_specs=[VMEM] * count,
        out_shape=[plain] * first + [coded] * (count - first),
        compiler_params=PARAMS,
        name="merge",
    )(kept, *arrived)


def total_kernel(stations, comps, counts, *refs):
    refs, o_ref = list(refs[:-1]), refs[-1]
    per_station = G * COMPS * COMPS
    for of, count in zip(comps, counts):
        own_ref, parts, refs = refs[0], refs[1:count], refs[count:]
        size = own_ref.shape[0]
        factors = [factor_of(part, size, 0) for part in parts]
        at = 0
        for g in range(G):
            for a in of:
                for b in range(COMPS):
                    rows = pl.ds(at, stations)
                    at += stations
                    value = own_ref[rows, :]
                    for part, factor in zip(parts, factors):
                        value = value + part[rows, :] * factor
                    o_ref[pl.ds((a * COMPS + b) * G + g, stations, stride=per_station), :] = value


def total(stations, comps, parts):
    counts = [len(of) for of in parts]
    return pl.pallas_call(
        functools.partial(total_kernel, stations, comps, counts),
        in_specs=[VMEM] * sum(counts),
        out_specs=VMEM,
        out_shape=jax.ShapeDtypeStruct((stations * COMPS * COMPS * G, LAG), f32),
        compiler_params=PARAMS,
        name="total",
    )(*[part for of in parts for part in of])


def swap(value, axis, mask):
    size = lax.axis_size(axis)
    return lax.ppermute(value, axis, [(i, i ^ mask) for i in range(size)])


def send(coded, mask):
    return swap(coded.astype(f16), "day", mask).astype(f32)


def owned_block(owner):
    ids = jnp.arange(owner.shape[0], dtype=jnp.int32)
    return jnp.sum(ids[None, :] * (owner[None, :] == ids[:, None]).astype(jnp.int32), axis=1)


def local(spectra, src_block, group_of, owner):
    stations = spectra.shape[3]
    days = lax.axis_size("day")
    ids = jnp.stack([lax.axis_index("day"), lax.axis_index("sta")])
    recv, signs, scale = receivers_by_freq(ids, spectra, group_of)
    columns = COMPS * stations
    table = jnp.asarray(lag_table(F, LAG))
    block_rows = S * stations // days

    if days == S and lax.axis_size("sta") == 4:
        y_first, z_first = (0, 1), (2,)
        ys, zs = [0, 1], range(0, days, 2)
        early, late = first_block(spectra, (z_first, y_first))
        far = swap(early, "sta", 2)
        beside, late = lax.optimization_barrier((swap(early, "sta", 1), late))
        far_late = swap(late, "sta", 2)
        far, recv, signs, scale, table = lax.optimization_barrier((far, recv, signs, scale, table))
        early = [early, beside, far, swap(far, "sta", 1)]
        pairs = [(mask, a) for mask in range(days) for a in z_first]
        cross = cross_spectra(pairs, z_first, ids, src_block, owner, recv, signs, early)
        kept_z, *away_z = lag_transform(
            [(False, [(y, z_first) for y in ys])] + [(True, [(y ^ z, z_first) for y in ys]) for z in zs[1:]],
            pairs,
            columns,
            cross,
            table,
            scale,
        )
        far_late, kept_z, away_z = lax.optimization_barrier((far_late, kept_z, away_z))
        late = [late, swap(late, "sta", 1), far_late, swap(far_late, "sta", 1)]
        pairs = [(mask, a) for mask in range(days) for a in y_first]
        cross = cross_spectra(pairs, y_first, ids, src_block, owner, recv, signs, late)
        lags = functools.partial(lag_transform, pairs=pairs, columns=columns, cross=cross, table=table, scale=scale)
        near, far = zs[: len(zs) // 2], zs[len(zs) // 2 :][::-1]
        (away_far,) = lags([(True, [(1 ^ z, y_first) for z in far])])
        arrived_far = send(away_far, 1)
        (away_near,) = lags([(True, [(1 ^ z, y_first) for z in near])])
        arrived_near = send(away_near, 1)
        arrived_z = [send(away_z[j], zs[1 + j]) for j in (0, 2, 1)]
        kept_near, kept_far = lags([(False, [(z, y_first) for z in of]) for of in (near, far)])
        merged = merge(kept_far, [arrived_far], len(far), 0)
        parts_far = [send(part, z) for part, z in zip(merged, far)]
        own_y, *merged = merge(kept_near, [arrived_near], len(near), 1)
        parts_y = [own_y] + [send(part, z) for part, z in zip(merged, near[1:])] + parts_far
        own_z, other = merge(kept_z, arrived_z, len(ys), 1)
        result = total(stations, (y_first, z_first), (parts_y, [own_z, send(other, 1)]))
        result = result.reshape(block_rows, COMPS * COMPS, G, LAG).transpose(0, 2, 1, 3)
        return result[None]

    every = tuple(range(COMPS))
    (first,) = first_block(spectra, (every,))
    gathered = lax.all_gather(first, "sta")
    blocks = [lax.dynamic_index_in_dim(gathered, src_block[k], 0, keepdims=False) for k in range(2)]
    order = jnp.arange(S, dtype=jnp.int32)
    pairs = [(mask, a) for mask in range(S) for a in every]
    cross = cross_spectra(pairs, every, jnp.zeros(2, jnp.int32), order[:2], order, recv, signs, blocks)
    outputs = [(False, [(mask, every) for mask in range(S)])]
    (partial,) = lag_transform(outputs, pairs, columns, cross, table, scale)
    partial = partial.reshape(S, G, COMPS * COMPS, stations, LAG).transpose(0, 3, 1, 2, 4)
    partial = partial.reshape(days, block_rows, G, COMPS * COMPS, LAG)
    ordered = jnp.take(partial, owned_block(owner), axis=0)
    return lax.psum_scatter(ordered, "day", scatter_dimension=0, tiled=True)


def solution(mesh):
    return jax.shard_map(
        local,
        mesh=mesh,
        in_specs=(P("day", None, None, "sta", None), P(), P(), P()),
        out_specs=P("day", "sta", None, None, None),
        check_vma=False,
    )
```

```python
import functools

import jax
import jax.numpy as jnp
import numpy as np
from jax import lax
from jax.experimental import pallas as pl
from jax.experimental.pallas import tpu as pltpu
from jax.sharding import PartitionSpec as P

F = 128
LAG = 128
G = 2
SB = 4
S = 8
COMPS = 3
XF = F + 8
XS = 2 * F + 8

f32 = jnp.float32
bf16 = jnp.bfloat16
f16 = jnp.float16
TAIL = 8
TOP = 14
PARAMS = pltpu.CompilerParams(vmem_limit_bytes=24 << 20)
VMEM = pl.BlockSpec(memory_space=pltpu.VMEM)
SMEM = pl.BlockSpec(memory_space=pltpu.SMEM)


def lag_table(freqs, lags):
    freq_ids = np.arange(freqs)
    lag_ids = np.arange(lags) - lags // 2
    angle = 2.0 * np.pi / (2 * freqs) * np.mod(freq_ids[:, None] * lag_ids[None, :], 2 * freqs)
    weight = np.where(freq_ids == 0, 1.0, 2.0)[:, None] / np.sqrt(freqs)
    return np.concatenate([weight * np.cos(angle), -weight * np.sin(angle)], axis=0).astype(np.float32)


def two_terms(value):
    high = value.astype(bf16)
    return high, (value - high.astype(f32)).astype(bf16)


def first_kernel(shares, x_ref, *refs):
    o_refs, wide = refs[:-1], refs[-1]
    rows = x_ref.shape[0] * 2
    for a in range(COMPS):
        for part in range(2):
            wide[a, part] = x_ref[:, part, a, 0:8].astype(f32)
        flat = wide.at[a].reshape(rows * 8, F)
        for of, o_ref in zip(shares, o_refs):
            if a in of:
                for s in range(SB):
                    o_ref[of.index(a), s] = flat[pl.ds(s, rows, stride=8), :].T.astype(bf16)


def first_block(spectra, shares):
    segs = spectra.shape[0]
    return pl.pallas_call(
        functools.partial(first_kernel, shares),
        in_specs=[VMEM],
        out_specs=[VMEM] * len(shares),
        out_shape=[jax.ShapeDtypeStruct((len(of), SB, F, 2 * segs), bf16) for of in shares],
        scratch_shapes=[pltpu.VMEM((COMPS, 2, segs, 8, F), f32)],
        compiler_params=PARAMS,
        name="first_block",
    )(spectra)


def receivers_kernel(ids_ref, x_ref, group_ref, o_ref, signs_ref, scale_ref, wide, turned):
    b = pl.program_id(0)
    rows = x_ref.shape[0] * 2
    stations = x_ref.shape[3]
    for part in range(2):
        wide[part] = x_ref[:, part, 0].astype(f32)
    flat = wide.reshape(rows * stations, F)
    for r in range(stations):
        turned[pl.ds(b * stations + r, F, stride=COMPS * stations), :] = flat[pl.ds(r, rows, stride=stations), :].T

    @pl.when(b == 0)
    def _():
        at = ids_ref[0] * (rows // 2)
        row = group_ref[pl.ds(at // rows, 1), :].astype(f32)
        swapped = pltpu.roll(row, rows // 2, 1)
        low = lax.broadcasted_iota(jnp.int32, row.shape, 1) < rows // 2
        mine = jnp.where(low == (at % rows == 0), row, swapped)
        for g in range(G):
            hot = jnp.where(mine == g, np.float32(1.0), np.float32(0.0))
            signs_ref[g : g + 1] = hot
            signs_ref[G + g : G + g + 1] = jnp.where(low, -hot, hot)
            hits = jnp.where(group_ref[...] == g, np.float32(1.0), np.float32(0.0))
            count = jnp.sum(hits, axis=(0, 1), keepdims=True)
            scale_ref[g : g + 1] = jnp.broadcast_to(1.0 / jnp.sqrt(count), (1, LAG))

    @pl.when(b == COMPS - 1)
    def _():
        def body(f, carry):
            o_ref[f] = turned[pl.ds(pl.multiple_of(f * COMPS * stations, 8), COMPS * stations), :].astype(bf16)
            return carry

        lax.fori_loop(0, F, body, 0, unroll=8)


def receivers_by_freq(ids, spectra, group_of):
    segs, stations = spectra.shape[0], spectra.shape[3]
    columns = COMPS * stations
    groups = group_of.reshape(-1, 2 * segs)
    fixed = lambda b: (0, 0)
    return pl.pallas_call(
        receivers_kernel,
        grid=(COMPS,),
        in_specs=[
            SMEM,
            pl.BlockSpec((segs, 2, 1, stations, F), lambda b: (0, 0, b, 0, 0)),
            pl.BlockSpec(groups.shape, fixed),
        ],
        out_specs=[
            pl.BlockSpec((F, columns, 2 * segs), lambda b: (0, 0, 0)),
            pl.BlockSpec((2 * G, 2 * segs), fixed),
            pl.BlockSpec((G, LAG), fixed),
        ],
        out_shape=[
            jax.ShapeDtypeStruct((F, columns, 2 * segs), bf16),
            jax.ShapeDtypeStruct((2 * G, 2 * segs), f32),
            jax.ShapeDtypeStruct((G, LAG), f32),
        ],
        scratch_shapes=[pltpu.VMEM((2, segs, stations, F), f32), pltpu.VMEM((F * columns, 2 * segs), f32)],
        compiler_params=PARAMS,
        cost_estimate=pl.CostEstimate(flops=0, bytes_accessed=12 << 20, transcendentals=0),
        name="receivers_by_freq",
    )(ids, spectra, groups)


def power_of_two(n):
    size = jnp.abs(n)
    result = jnp.ones(n.shape, f32)
    for i in range(7):
        factor = jnp.where(n < 0, np.float32(2.0 ** -(2**i)), np.float32(2.0 ** (2**i)))
        result = result * jnp.where((size >> i) & 1 == 1, factor, np.float32(1.0))
    return result


def exponent_of(value):
    largest = jnp.max(jnp.abs(value), axis=(0, 1), keepdims=True)
    return jnp.ceil(jnp.log(jnp.maximum(largest, 1e-30)) * np.float32(1.4426950408889634)).astype(jnp.int32)


def rows_of(comps):
    return -(-S * len(comps) // 8) * 8


def cross_kernel(comps, ids_ref, src_block_ref, owner_ref, recv_ref, signs_ref, *rest):
    blocks, (o_ref, src) = rest[:-2], rest[-2:]
    rows = rows_of(comps)
    columns = recv_ref.shape[1]
    half = recv_ref.shape[2] // 2
    for k in range(S // SB):
        which = ids_ref[1] ^ src_block_ref[k]
        for j in range(len(blocks)):

            @pl.when(which == j)
            def _():
                for station in range(SB):
                    mask = ids_ref[0] ^ owner_ref[k * SB + station]
                    for a in range(len(comps)):
                        src[mask * len(comps) + a, 0:F] = blocks[j][a, station].astype(f32)

    flat = src.reshape(rows * XF, src.shape[2])
    signs = signs_ref[...]

    def one_freq(f, carry):
        plain = flat[pl.ds(f, rows, stride=XF), :]
        rolled = pltpu.roll(plain, half, 1)
        left = [plain * signs[0:1], plain * signs[1:2], rolled * signs[2:3], rolled * signs[3:4]]
        left = jnp.concatenate(left, axis=0).astype(bf16)
        out = lax.dot_general(left, recv_ref[f], (((1,), (1,)), ((), ())), preferred_element_type=f32)
        o_ref[pl.ds(f, G * rows, stride=XS), 0:columns] = out[: G * rows]
        o_ref[pl.ds(F + f, G * rows, stride=XS), 0:columns] = out[G * rows :]
        return carry

    lax.fori_loop(0, F, one_freq, 0, unroll=F)


def cross_spectra(comps, ids, src_block, owner, recv, signs, blocks):
    depth = recv.shape[2]
    rows = rows_of(comps)
    return pl.pallas_call(
        functools.partial(cross_kernel, comps),
        in_specs=[SMEM] * 3 + [VMEM] * (2 + len(blocks)),
        out_specs=VMEM,
        out_shape=jax.ShapeDtypeStruct((G * rows * XS, 128), f32),
        scratch_shapes=[pltpu.VMEM((rows, XF, depth), f32)],
        compiler_params=PARAMS,
        cost_estimate=pl.CostEstimate(flops=0, bytes_accessed=10 << 20, transcendentals=0),
        name="cross_spectra",
    )(ids, src_block, owner, recv, signs, *blocks)


def lag_kernel(outputs, held, columns, cross_ref, table_ref, scale_ref, *o_refs):
    rows = rows_of(held)
    table_high, table_low = two_terms(table_ref[...])
    table = jnp.concatenate([table_high, table_low], axis=1)
    for (coded, blocks_of), o_ref in zip(outputs, o_refs):
        exponents = jnp.zeros((TAIL, LAG), f32)
        done = 0
        for at, (mask, comps) in enumerate(blocks_of):
            turned = []
            for g in range(G):
                for a in comps:
                    first = (g * rows + mask * len(held) + held.index(a)) * XS
                    turned.append(cross_ref[first : first + 2 * F, :].T[:columns])
            high, low = two_terms(jnp.concatenate(turned, axis=0))
            both = jnp.dot(high, table, preferred_element_type=f32)
            lagged = both[:, :LAG] + both[:, LAG:] + jnp.dot(low, table_high, preferred_element_type=f32)
            part = len(comps) * columns
            lagged = [lagged[g * part : (g + 1) * part] * scale_ref[g : g + 1] for g in range(G)]
            lagged = jnp.concatenate(lagged, axis=0)
            if coded:
                e = exponent_of(lagged)
                lagged = lagged * power_of_two(TOP - e)
                exponents = jnp.where(lax.broadcasted_iota(jnp.int32, (TAIL, LAG), 0) == at, e.astype(f32), exponents)
            o_ref[done : done + G * part] = lagged
            done += G * part
        if coded:
            o_ref[done:] = exponents


def lag_transform(outputs, held, columns, cross, table, scale):
    shapes = []
    for coded, blocks_of in outputs:
        size = sum(G * len(comps) * columns for _, comps in blocks_of) + (TAIL if coded else 0)
        shapes.append(jax.ShapeDtypeStruct((size, LAG), f32))
    return pl.pallas_call(
        functools.partial(lag_kernel, outputs, held, columns),
        in_specs=[VMEM] * 3,
        out_specs=[VMEM] * len(outputs),
        out_shape=shapes,
        compiler_params=PARAMS,
        cost_estimate=pl.CostEstimate(flops=0, bytes_accessed=5 << 20, transcendentals=0),
        name="lag_transform",
    )(cross, table, scale)


def factor_of(coded_ref, at):
    return power_of_two(coded_ref[at : at + 1, 0:1].astype(jnp.int32) - TOP)


def merge_kernel(counts, outputs, *refs):
    sums, o_refs = refs[: 2 * len(counts)], refs[2 * len(counts) :]
    for (coded, blocks_of), o_ref in zip(outputs, o_refs):
        exponents = jnp.zeros((TAIL, LAG), f32)
        done = 0
        for at, (i, j) in enumerate(blocks_of):
            kept_ref, arrived_ref = sums[2 * i : 2 * i + 2]
            size = kept_ref.shape[0] // counts[i]
            rows = slice(j * size, (j + 1) * size)
            value = kept_ref[rows] + arrived_ref[rows] * factor_of(arrived_ref, counts[i] * size + j)
            if coded:
                e = exponent_of(value)
                value = value * power_of_two(TOP - e)
                exponents = jnp.where(lax.broadcasted_iota(jnp.int32, (TAIL, LAG), 0) == at, e.astype(f32), exponents)
            o_ref[done : done + size] = value
            done += size
        if coded:
            o_ref[done:] = exponents


def merge(sums, outputs):
    shapes = []
    for coded, blocks_of in outputs:
        size = sum(sums[i][1].shape[0] // sums[i][0] for i, _ in blocks_of) + (TAIL if coded else 0)
        shapes.append(jax.ShapeDtypeStruct((size, LAG), f32))
    return pl.pallas_call(
        functools.partial(merge_kernel, [count for count, _, _ in sums], outputs),
        in_specs=[VMEM] * (2 * len(sums)),
        out_specs=[VMEM] * len(outputs),
        out_shape=shapes,
        compiler_params=PARAMS,
        name="merge",
    )(*[array for _, *arrays in sums for array in arrays])


def total_kernel(stations, terms, *refs):
    refs, o_ref = refs[:-1], refs[-1]
    per_station = G * COMPS * COMPS
    for comps, parts in terms:
        factors = [None if at is None else factor_of(refs[i], at) for i, _, at in parts]
        done = 0
        for g in range(G):
            for a in comps:
                for b in range(COMPS):
                    value = None
                    for (i, first, _), factor in zip(parts, factors):
                        part = refs[i][first + done : first + done + stations, :]
                        part = part if factor is None else part * factor
                        value = part if value is None else value + part
                    done += stations
                    o_ref[pl.ds((a * COMPS + b) * G + g, stations, stride=per_station), :] = value


def total(stations, terms, arrays):
    return pl.pallas_call(
        functools.partial(total_kernel, stations, terms),
        in_specs=[VMEM] * len(arrays),
        out_specs=VMEM,
        out_shape=jax.ShapeDtypeStruct((stations * COMPS * COMPS * G, LAG), f32),
        compiler_params=PARAMS,
        name="total",
    )(*arrays)


def swap(value, axis, mask):
    size = lax.axis_size(axis)
    return lax.ppermute(value, axis, [(i, i ^ mask) for i in range(size)])


def send(coded, mask):
    return swap(coded.astype(f16), "day", mask).astype(f32)


def owned_block(owner):
    ids = jnp.arange(owner.shape[0], dtype=jnp.int32)
    return jnp.sum(ids[None, :] * (owner[None, :] == ids[:, None]).astype(jnp.int32), axis=1)


def local(spectra, src_block, group_of, owner):
    stations = spectra.shape[3]
    days = lax.axis_size("day")
    ids = jnp.stack([lax.axis_index("day"), lax.axis_index("sta")])
    recv, signs, scale = receivers_by_freq(ids, spectra, group_of)
    columns = COMPS * stations
    table = jnp.asarray(lag_table(F, LAG))
    block_rows = S * stations // days

    if days == S and lax.axis_size("sta") == 4:
        ahead, rest = (2,), (0, 1)
        near, far = [0, 2], [6, 4]
        early, late = first_block(spectra, (ahead, rest))
        across = swap(early, "sta", 2)
        beside, late = lax.optimization_barrier((swap(early, "sta", 1), late))
        across_late = swap(late, "sta", 2)
        across, recv, signs, scale, table = lax.optimization_barrier((across, recv, signs, scale, table))
        early = [early, beside, across, swap(across, "sta", 1)]
        cross = cross_spectra(ahead, ids, src_block, owner, recv, signs, early)
        away, kept = lag_transform(
            [(True, [(1 ^ z, ahead) for z in near + far]), (False, [(z, ahead) for z in near + far])],
            ahead,
            columns,
            cross,
            table,
            scale,
        )
        across_late, away, kept = lax.optimization_barrier((across_late, away, kept))
        arrived = send(away, 1)
        late = [late, swap(late, "sta", 1), across_late, swap(across_late, "sta", 1)]
        cross = cross_spectra(rest, ids, src_block, owner, recv, signs, late)
        lags = functools.partial(lag_transform, held=rest, columns=columns, cross=cross, table=table, scale=scale)
        (away_far,) = lags([(True, [(1 ^ z, rest) for z in far])])
        away_far, cross = lax.optimization_barrier((away_far, cross))
        arrived_far = send(away_far, 1)
        (away_near,) = lags([(True, [(1 ^ z, rest) for z in near])], cross=cross)
        arrived_near = send(away_near, 1)
        kept, away = merge([(4, kept, arrived)], [(False, [(0, 0), (0, 1)]), (True, [(0, 3), (0, 2)])])
        arrived = send(away, 4)
        kept_near, kept_far = lags([(False, [(z, rest) for z in of]) for of in (near, far)], cross=cross)
        by_6, by_4 = merge([(2, kept_far, arrived_far)], [(True, [(0, 0)]), (True, [(0, 1)])])
        kept_near, by_6, by_4 = lax.optimization_barrier((kept_near, by_6, by_4))
        by_6 = send(by_6, 6)
        by_4 = send(by_4, 4)
        own_rest, by_2 = merge([(2, kept_near, arrived_near)], [(False, [(0, 0)]), (True, [(0, 1)])])
        by_2 = send(by_2, 2)
        own_ahead, ahead_by_2 = merge([(2, kept, arrived)], [(False, [(0, 0)]), (True, [(0, 1)])])
        ahead_by_2 = send(ahead_by_2, 2)
        size, ahead_size = own_rest.shape[0], own_ahead.shape[0]
        terms = [
            (rest, [(0, 0, None), (1, 0, size), (2, 0, size), (3, 0, size)]),
            (ahead, [(4, 0, None), (5, 0, ahead_size)]),
        ]
        result = total(stations, terms, [own_rest, by_2, by_6, by_4, own_ahead, ahead_by_2])
        result = result.reshape(block_rows, COMPS * COMPS, G, LAG).transpose(0, 2, 1, 3)
        return result[None]

    every = tuple(range(COMPS))
    (first,) = first_block(spectra, (every,))
    gathered = lax.all_gather(first, "sta")
    blocks = [lax.dynamic_index_in_dim(gathered, src_block[k], 0, keepdims=False) for k in range(2)]
    order = jnp.arange(S, dtype=jnp.int32)
    cross = cross_spectra(every, jnp.zeros(2, jnp.int32), order[:2], order, recv, signs, blocks)
    outputs = [(False, [(mask, every) for mask in range(S)])]
    (partial,) = lag_transform(outputs, every, columns, cross, table, scale)
    partial = partial.reshape(S, G, COMPS * COMPS, stations, LAG).transpose(0, 3, 1, 2, 4)
    partial = partial.reshape(days, block_rows, G, COMPS * COMPS, LAG)
    ordered = jnp.take(partial, owned_block(owner), axis=0)
    return lax.psum_scatter(ordered, "day", scatter_dimension=0, tiled=True)


def solution(mesh):
    return jax.shard_map(
        local,
        mesh=mesh,
        in_specs=(P("day", None, None, "sta", None), P(), P(), P()),
        out_specs=P("day", "sta", None, None, None),
        check_vma=False,
    )
```

```python
import functools

import jax
import jax.numpy as jnp
import numpy as np
from jax import lax
from jax.experimental import pallas as pl
from jax.experimental.pallas import tpu as pltpu
from jax.sharding import PartitionSpec as P

F = 128
LAG = 128
G = 2
SB = 4
S = 8
COMPS = 3
XF = F + 8
XS = 2 * F + 8

f32 = jnp.float32
bf16 = jnp.bfloat16
f16 = jnp.float16
TAIL = 8
TOP = 14
PARAMS = pltpu.CompilerParams(vmem_limit_bytes=24 << 20)
VMEM = pl.BlockSpec(memory_space=pltpu.VMEM)
SMEM = pl.BlockSpec(memory_space=pltpu.SMEM)


def lag_table(freqs, lags):
    freq_ids = np.arange(freqs)
    lag_ids = np.arange(lags) - lags // 2
    angle = 2.0 * np.pi / (2 * freqs) * np.mod(freq_ids[:, None] * lag_ids[None, :], 2 * freqs)
    weight = np.where(freq_ids == 0, 1.0, 2.0)[:, None] / np.sqrt(freqs)
    return np.concatenate([weight * np.cos(angle), -weight * np.sin(angle)], axis=0).astype(np.float32)


def two_terms(value):
    high = value.astype(bf16)
    return high, (value - high.astype(f32)).astype(bf16)


def first_kernel(shares, x_ref, *refs):
    o_refs, wide = refs[:-1], refs[-1]
    rows = x_ref.shape[0] * 2
    for a in range(COMPS):
        for part in range(2):
            wide[a, part] = x_ref[:, part, a, 0:8].astype(f32)
        flat = wide.at[a].reshape(rows * 8, F)
        for of, o_ref in zip(shares, o_refs):
            if a in of:
                for s in range(SB):
                    o_ref[of.index(a), s] = flat[pl.ds(s, rows, stride=8), :].T.astype(bf16)


def first_block(spectra, shares):
    segs = spectra.shape[0]
    return pl.pallas_call(
        functools.partial(first_kernel, shares),
        in_specs=[VMEM],
        out_specs=[VMEM] * len(shares),
        out_shape=[jax.ShapeDtypeStruct((len(of), SB, F, 2 * segs), bf16) for of in shares],
        scratch_shapes=[pltpu.VMEM((COMPS, 2, segs, 8, F), f32)],
        compiler_params=PARAMS,
        name="first_block",
    )(spectra)


def receivers_kernel(ids_ref, x_ref, group_ref, o_ref, signs_ref, scale_ref, wide, turned):
    b = pl.program_id(0)
    rows = x_ref.shape[0] * 2
    stations = x_ref.shape[3]
    for part in range(2):
        wide[part] = x_ref[:, part, 0].astype(f32)
    flat = wide.reshape(rows * stations, F)
    for r in range(stations):
        turned[pl.ds(b * stations + r, F, stride=COMPS * stations), :] = flat[pl.ds(r, rows, stride=stations), :].T

    @pl.when(b == 0)
    def _():
        at = ids_ref[0] * (rows // 2)
        row = group_ref[pl.ds(at // rows, 1), :].astype(f32)
        swapped = pltpu.roll(row, rows // 2, 1)
        low = lax.broadcasted_iota(jnp.int32, row.shape, 1) < rows // 2
        mine = jnp.where(low == (at % rows == 0), row, swapped)
        for g in range(G):
            hot = jnp.where(mine == g, np.float32(1.0), np.float32(0.0))
            signs_ref[g : g + 1] = hot
            signs_ref[G + g : G + g + 1] = jnp.where(low, -hot, hot)
            hits = jnp.where(group_ref[...] == g, np.float32(1.0), np.float32(0.0))
            count = jnp.sum(hits, axis=(0, 1), keepdims=True)
            scale_ref[g : g + 1] = jnp.broadcast_to(1.0 / jnp.sqrt(count), (1, LAG))

    @pl.when(b == COMPS - 1)
    def _():
        def body(f, carry):
            o_ref[f] = turned[pl.ds(pl.multiple_of(f * COMPS * stations, 8), COMPS * stations), :].astype(bf16)
            return carry

        lax.fori_loop(0, F, body, 0, unroll=8)


def receivers_by_freq(ids, spectra, group_of):
    segs, stations = spectra.shape[0], spectra.shape[3]
    columns = COMPS * stations
    groups = group_of.reshape(-1, 2 * segs)
    fixed = lambda b: (0, 0)
    return pl.pallas_call(
        receivers_kernel,
        grid=(COMPS,),
        in_specs=[
            SMEM,
            pl.BlockSpec((segs, 2, 1, stations, F), lambda b: (0, 0, b, 0, 0)),
            pl.BlockSpec(groups.shape, fixed),
        ],
        out_specs=[
            pl.BlockSpec((F, columns, 2 * segs), lambda b: (0, 0, 0)),
            pl.BlockSpec((2 * G, 2 * segs), fixed),
            pl.BlockSpec((G, LAG), fixed),
        ],
        out_shape=[
            jax.ShapeDtypeStruct((F, columns, 2 * segs), bf16),
            jax.ShapeDtypeStruct((2 * G, 2 * segs), f32),
            jax.ShapeDtypeStruct((G, LAG), f32),
        ],
        scratch_shapes=[pltpu.VMEM((2, segs, stations, F), f32), pltpu.VMEM((F * columns, 2 * segs), f32)],
        compiler_params=PARAMS,
        cost_estimate=pl.CostEstimate(flops=0, bytes_accessed=12 << 20, transcendentals=0),
        name="receivers_by_freq",
    )(ids, spectra, groups)


def power_of_two(n):
    size = jnp.abs(n)
    result = jnp.ones(n.shape, f32)
    for i in range(7):
        factor = jnp.where(n < 0, np.float32(2.0 ** -(2**i)), np.float32(2.0 ** (2**i)))
        result = result * jnp.where((size >> i) & 1 == 1, factor, np.float32(1.0))
    return result


def exponent_of(value):
    largest = jnp.max(jnp.abs(value), axis=(0, 1), keepdims=True)
    return jnp.ceil(jnp.log(jnp.maximum(largest, 1e-30)) * np.float32(1.4426950408889634)).astype(jnp.int32)


def rows_of(comps):
    return -(-S * len(comps) // 8) * 8


def cross_kernel(comps, ids_ref, src_block_ref, owner_ref, recv_ref, signs_ref, *rest):
    blocks, (o_ref, src) = rest[:-2], rest[-2:]
    rows = rows_of(comps)
    columns = recv_ref.shape[1]
    half = recv_ref.shape[2] // 2
    for k in range(S // SB):
        which = ids_ref[1] ^ src_block_ref[k]
        for j in range(len(blocks)):

            @pl.when(which == j)
            def _():
                for station in range(SB):
                    mask = ids_ref[0] ^ owner_ref[k * SB + station]
                    for a in range(len(comps)):
                        src[mask * len(comps) + a, 0:F] = blocks[j][a, station].astype(f32)

    flat = src.reshape(rows * XF, src.shape[2])
    signs = signs_ref[...]

    def one_freq(f, carry):
        plain = flat[pl.ds(f, rows, stride=XF), :]
        rolled = pltpu.roll(plain, half, 1)
        left = [plain * signs[0:1], plain * signs[1:2], rolled * signs[2:3], rolled * signs[3:4]]
        left = jnp.concatenate(left, axis=0).astype(bf16)
        out = lax.dot_general(left, recv_ref[f], (((1,), (1,)), ((), ())), preferred_element_type=f32)
        o_ref[pl.ds(f, G * rows, stride=XS), 0:columns] = out[: G * rows]
        o_ref[pl.ds(F + f, G * rows, stride=XS), 0:columns] = out[G * rows :]
        return carry

    lax.fori_loop(0, F, one_freq, 0, unroll=F)


def cross_spectra(comps, ids, src_block, owner, recv, signs, blocks):
    depth = recv.shape[2]
    rows = rows_of(comps)
    return pl.pallas_call(
        functools.partial(cross_kernel, comps),
        in_specs=[SMEM] * 3 + [VMEM] * (2 + len(blocks)),
        out_specs=VMEM,
        out_shape=jax.ShapeDtypeStruct((G * rows * XS, 128), f32),
        scratch_shapes=[pltpu.VMEM((rows, XF, depth), f32)],
        compiler_params=PARAMS,
        cost_estimate=pl.CostEstimate(flops=0, bytes_accessed=10 << 20, transcendentals=0),
        name="cross_spectra",
    )(ids, src_block, owner, recv, signs, *blocks)


def lag_kernel(outputs, held, columns, cross_ref, table_ref, scale_ref, *o_refs):
    rows = rows_of(held)
    table_high, table_low = two_terms(table_ref[...])
    table = jnp.concatenate([table_high, table_low], axis=1)
    for (coded, blocks_of), o_ref in zip(outputs, o_refs):
        exponents = jnp.zeros((TAIL, LAG), f32)
        done = 0
        for at, (mask, comps) in enumerate(blocks_of):
            turned = []
            for g in range(G):
                for a in comps:
                    first = (g * rows + mask * len(held) + held.index(a)) * XS
                    turned.append(cross_ref[first : first + 2 * F, :].T[:columns])
            high, low = two_terms(jnp.concatenate(turned, axis=0))
            both = jnp.dot(high, table, preferred_element_type=f32)
            lagged = both[:, :LAG] + both[:, LAG:] + jnp.dot(low, table_high, preferred_element_type=f32)
            part = len(comps) * columns
            lagged = [lagged[g * part : (g + 1) * part] * scale_ref[g : g + 1] for g in range(G)]
            lagged = jnp.concatenate(lagged, axis=0)
            if coded:
                e = exponent_of(lagged)
                lagged = lagged * power_of_two(TOP - e)
                exponents = jnp.where(lax.broadcasted_iota(jnp.int32, (TAIL, LAG), 0) == at, e.astype(f32), exponents)
            o_ref[done : done + G * part] = lagged
            done += G * part
        if coded:
            o_ref[done:] = exponents


def lag_transform(outputs, held, columns, cross, table, scale):
    shapes = []
    for coded, blocks_of in outputs:
        size = sum(G * len(comps) * columns for _, comps in blocks_of) + (TAIL if coded else 0)
        shapes.append(jax.ShapeDtypeStruct((size, LAG), f32))
    return pl.pallas_call(
        functools.partial(lag_kernel, outputs, held, columns),
        in_specs=[VMEM] * 3,
        out_specs=[VMEM] * len(outputs),
        out_shape=shapes,
        compiler_params=PARAMS,
        cost_estimate=pl.CostEstimate(flops=0, bytes_accessed=5 << 20, transcendentals=0),
        name="lag_transform",
    )(cross, table, scale)


def factor_of(coded_ref, at):
    return power_of_two(coded_ref[at : at + 1, 0:1].astype(jnp.int32) - TOP)


def merge_kernel(counts, outputs, *refs):
    sums, o_refs = refs[: 2 * len(counts)], refs[2 * len(counts) :]
    for (coded, blocks_of), o_ref in zip(outputs, o_refs):
        exponents = jnp.zeros((TAIL, LAG), f32)
        done = 0
        for at, (i, j) in enumerate(blocks_of):
            kept_ref, arrived_ref = sums[2 * i : 2 * i + 2]
            size = kept_ref.shape[0] // counts[i]
            rows = slice(j * size, (j + 1) * size)
            value = kept_ref[rows] + arrived_ref[rows] * factor_of(arrived_ref, counts[i] * size + j)
            if coded:
                e = exponent_of(value)
                value = value * power_of_two(TOP - e)
                exponents = jnp.where(lax.broadcasted_iota(jnp.int32, (TAIL, LAG), 0) == at, e.astype(f32), exponents)
            o_ref[done : done + size] = value
            done += size
        if coded:
            o_ref[done:] = exponents


def merge(sums, outputs):
    shapes = []
    for coded, blocks_of in outputs:
        size = sum(sums[i][1].shape[0] // sums[i][0] for i, _ in blocks_of) + (TAIL if coded else 0)
        shapes.append(jax.ShapeDtypeStruct((size, LAG), f32))
    return pl.pallas_call(
        functools.partial(merge_kernel, [count for count, _, _ in sums], outputs),
        in_specs=[VMEM] * (2 * len(sums)),
        out_specs=[VMEM] * len(outputs),
        out_shape=shapes,
        compiler_params=PARAMS,
        name="merge",
    )(*[array for _, *arrays in sums for array in arrays])


def total_kernel(stations, terms, *refs):
    refs, o_ref = refs[:-1], refs[-1]
    per_station = G * COMPS * COMPS
    for comps, parts in terms:
        factors = [None if at is None else factor_of(refs[i], at) for i, _, at in parts]
        done = 0
        for g in range(G):
            for a in comps:
                for b in range(COMPS):
                    value = None
                    for (i, first, _), factor in zip(parts, factors):
                        part = refs[i][first + done : first + done + stations, :]
                        part = part if factor is None else part * factor
                        value = part if value is None else value + part
                    done += stations
                    o_ref[pl.ds((a * COMPS + b) * G + g, stations, stride=per_station), :] = value


def total(stations, terms, arrays):
    return pl.pallas_call(
        functools.partial(total_kernel, stations, terms),
        in_specs=[VMEM] * len(arrays),
        out_specs=VMEM,
        out_shape=jax.ShapeDtypeStruct((stations * COMPS * COMPS * G, LAG), f32),
        compiler_params=PARAMS,
        name="total",
    )(*arrays)


def swap(value, axis, mask):
    size = lax.axis_size(axis)
    return lax.ppermute(value, axis, [(i, i ^ mask) for i in range(size)])


def send(coded, mask):
    return swap(coded.astype(f16), "day", mask).astype(f32)


def owned_block(owner):
    ids = jnp.arange(owner.shape[0], dtype=jnp.int32)
    return jnp.sum(ids[None, :] * (owner[None, :] == ids[:, None]).astype(jnp.int32), axis=1)


def local(spectra, src_block, group_of, owner):
    stations = spectra.shape[3]
    days = lax.axis_size("day")
    ids = jnp.stack([lax.axis_index("day"), lax.axis_index("sta")])
    recv, signs, scale = receivers_by_freq(ids, spectra, group_of)
    columns = COMPS * stations
    table = jnp.asarray(lag_table(F, LAG))
    block_rows = S * stations // days

    if days == S and lax.axis_size("sta") == 4:
        ahead, rest = (2,), (0, 1)
        near, far = [0, 2], [6, 4]
        early, late = first_block(spectra, (ahead, rest))
        across = swap(early, "sta", 2)
        beside, late = lax.optimization_barrier((swap(early, "sta", 1), late))
        across_late = swap(late, "sta", 2)
        across, recv, signs, scale, table = lax.optimization_barrier((across, recv, signs, scale, table))
        early = [early, beside, across, swap(across, "sta", 1)]
        cross = cross_spectra(ahead, ids, src_block, owner, recv, signs, early)
        away, kept = lag_transform(
            [(True, [(1 ^ z, ahead) for z in near + far]), (False, [(z, ahead) for z in near + far])],
            ahead,
            columns,
            cross,
            table,
            scale,
        )
        across_late, away, kept = lax.optimization_barrier((across_late, away, kept))
        arrived = send(away, 1)
        late = [late, swap(late, "sta", 1), across_late, swap(across_late, "sta", 1)]
        cross = cross_spectra(rest, ids, src_block, owner, recv, signs, late)
        lags = functools.partial(lag_transform, held=rest, columns=columns, cross=cross, table=table, scale=scale)
        (away_far,) = lags([(True, [(1 ^ z, rest) for z in far])])
        away_far, cross = lax.optimization_barrier((away_far, cross))
        arrived_far = send(away_far, 1)
        (away_near,) = lags([(True, [(2, rest), (3, rest)])], cross=cross)
        arrived_near = send(away_near, 2)
        kept, away = merge([(4, kept, arrived)], [(False, [(0, 0), (0, 1)]), (True, [(0, 3), (0, 2)])])
        arrived = send(away, 4)
        kept_near, kept_far = lags([(False, [(z, rest) for z in of]) for of in ((0, 1), far)], cross=cross)
        by_6, by_4 = merge([(2, kept_far, arrived_far)], [(True, [(0, 0)]), (True, [(0, 1)])])
        kept_near, by_6, by_4 = lax.optimization_barrier((kept_near, by_6, by_4))
        by_6 = send(by_6, 6)
        by_4 = send(by_4, 4)
        own_rest, by_1 = merge([(2, kept_near, arrived_near)], [(False, [(0, 0)]), (True, [(0, 1)])])
        by_1 = send(by_1, 1)
        own_ahead, ahead_by_2 = merge([(2, kept, arrived)], [(False, [(0, 0)]), (True, [(0, 1)])])
        ahead_by_2 = send(ahead_by_2, 2)
        size, ahead_size = own_rest.shape[0], own_ahead.shape[0]
        terms = [
            (rest, [(0, 0, None), (1, 0, size), (2, 0, size), (3, 0, size)]),
            (ahead, [(4, 0, None), (5, 0, ahead_size)]),
        ]
        result = total(stations, terms, [own_rest, by_1, by_6, by_4, own_ahead, ahead_by_2])
        result = result.reshape(block_rows, COMPS * COMPS, G, LAG).transpose(0, 2, 1, 3)
        return result[None]

    every = tuple(range(COMPS))
    (first,) = first_block(spectra, (every,))
    gathered = lax.all_gather(first, "sta")
    blocks = [lax.dynamic_index_in_dim(gathered, src_block[k], 0, keepdims=False) for k in range(2)]
    order = jnp.arange(S, dtype=jnp.int32)
    cross = cross_spectra(every, jnp.zeros(2, jnp.int32), order[:2], order, recv, signs, blocks)
    outputs = [(False, [(mask, every) for mask in range(S)])]
    (partial,) = lag_transform(outputs, every, columns, cross, table, scale)
    partial = partial.reshape(S, G, COMPS * COMPS, stations, LAG).transpose(0, 3, 1, 2, 4)
    partial = partial.reshape(days, block_rows, G, COMPS * COMPS, LAG)
    ordered = jnp.take(partial, owned_block(owner), axis=0)
    return lax.psum_scatter(ordered, "day", scatter_dimension=0, tiled=True)


def solution(mesh):
    return jax.shard_map(
        local,
        mesh=mesh,
        in_specs=(P("day", None, None, "sta", None), P(), P(), P()),
        out_specs=P("day", "sta", None, None, None),
        check_vma=False,
    )
```

```python
import functools

import jax
import jax.numpy as jnp
import numpy as np
from jax import lax
from jax.experimental import pallas as pl
from jax.experimental.pallas import tpu as pltpu
from jax.sharding import PartitionSpec as P

F = 128
LAG = 128
G = 2
SB = 4
S = 8
COMPS = 3
XF = F + 8
XS = 2 * F + 8

f32 = jnp.float32
bf16 = jnp.bfloat16
f16 = jnp.float16
TAIL = 8
TOP = 14
PARAMS = pltpu.CompilerParams(vmem_limit_bytes=24 << 20)
VMEM = pl.BlockSpec(memory_space=pltpu.VMEM)
SMEM = pl.BlockSpec(memory_space=pltpu.SMEM)


def lag_table(freqs, lags):
    freq_ids = np.arange(freqs)
    lag_ids = np.arange(lags) - lags // 2
    angle = 2.0 * np.pi / (2 * freqs) * np.mod(freq_ids[:, None] * lag_ids[None, :], 2 * freqs)
    weight = np.where(freq_ids == 0, 1.0, 2.0)[:, None] / np.sqrt(freqs)
    return np.concatenate([weight * np.cos(angle), -weight * np.sin(angle)], axis=0).astype(np.float32)


def two_terms(value):
    high = value.astype(bf16)
    return high, (value - high.astype(f32)).astype(bf16)


def first_kernel(shares, x_ref, *refs):
    o_refs, wide = refs[:-1], refs[-1]
    rows = x_ref.shape[0] * 2
    for a in range(COMPS):
        for part in range(2):
            wide[a, part] = x_ref[:, part, a, 0:8].astype(f32)
        flat = wide.at[a].reshape(rows * 8, F)
        for of, o_ref in zip(shares, o_refs):
            if a in of:
                for s in range(SB):
                    o_ref[of.index(a), s] = flat[pl.ds(s, rows, stride=8), :].T.astype(bf16)


def first_block(spectra, shares):
    segs = spectra.shape[0]
    return pl.pallas_call(
        functools.partial(first_kernel, shares),
        in_specs=[VMEM],
        out_specs=[VMEM] * len(shares),
        out_shape=[jax.ShapeDtypeStruct((len(of), SB, F, 2 * segs), bf16) for of in shares],
        scratch_shapes=[pltpu.VMEM((COMPS, 2, segs, 8, F), f32)],
        compiler_params=PARAMS,
        name="first_block",
    )(spectra)


def receivers_kernel(ids_ref, x_ref, group_ref, o_ref, signs_ref, scale_ref, wide, turned):
    b = pl.program_id(0)
    rows = x_ref.shape[0] * 2
    stations = x_ref.shape[3]
    for part in range(2):
        wide[part] = x_ref[:, part, 0].astype(f32)
    flat = wide.reshape(rows * stations, F)
    for r in range(stations):
        turned[pl.ds(b * stations + r, F, stride=COMPS * stations), :] = flat[pl.ds(r, rows, stride=stations), :].T

    @pl.when(b == 0)
    def _():
        at = ids_ref[0] * (rows // 2)
        row = group_ref[pl.ds(at // rows, 1), :].astype(f32)
        swapped = pltpu.roll(row, rows // 2, 1)
        low = lax.broadcasted_iota(jnp.int32, row.shape, 1) < rows // 2
        mine = jnp.where(low == (at % rows == 0), row, swapped)
        for g in range(G):
            hot = jnp.where(mine == g, np.float32(1.0), np.float32(0.0))
            signs_ref[g : g + 1] = hot
            signs_ref[G + g : G + g + 1] = jnp.where(low, -hot, hot)
            hits = jnp.where(group_ref[...] == g, np.float32(1.0), np.float32(0.0))
            count = jnp.sum(hits, axis=(0, 1), keepdims=True)
            scale_ref[g : g + 1] = jnp.broadcast_to(1.0 / jnp.sqrt(count), (1, LAG))

    @pl.when(b == COMPS - 1)
    def _():
        def body(f, carry):
            o_ref[f] = turned[pl.ds(pl.multiple_of(f * COMPS * stations, 8), COMPS * stations), :].astype(bf16)
            return carry

        lax.fori_loop(0, F, body, 0, unroll=8)


def receivers_by_freq(ids, spectra, group_of):
    segs, stations = spectra.shape[0], spectra.shape[3]
    columns = COMPS * stations
    groups = group_of.reshape(-1, 2 * segs)
    fixed = lambda b: (0, 0)
    return pl.pallas_call(
        receivers_kernel,
        grid=(COMPS,),
        in_specs=[
            SMEM,
            pl.BlockSpec((segs, 2, 1, stations, F), lambda b: (0, 0, b, 0, 0)),
            pl.BlockSpec(groups.shape, fixed),
        ],
        out_specs=[
            pl.BlockSpec((F, columns, 2 * segs), lambda b: (0, 0, 0)),
            pl.BlockSpec((2 * G, 2 * segs), fixed),
            pl.BlockSpec((G, LAG), fixed),
        ],
        out_shape=[
            jax.ShapeDtypeStruct((F, columns, 2 * segs), bf16),
            jax.ShapeDtypeStruct((2 * G, 2 * segs), f32),
            jax.ShapeDtypeStruct((G, LAG), f32),
        ],
        scratch_shapes=[pltpu.VMEM((2, segs, stations, F), f32), pltpu.VMEM((F * columns, 2 * segs), f32)],
        compiler_params=PARAMS,
        cost_estimate=pl.CostEstimate(flops=0, bytes_accessed=12 << 20, transcendentals=0),
        name="receivers_by_freq",
    )(ids, spectra, groups)


def power_of_two(n):
    size = jnp.abs(n)
    result = jnp.ones(n.shape, f32)
    for i in range(7):
        factor = jnp.where(n < 0, np.float32(2.0 ** -(2**i)), np.float32(2.0 ** (2**i)))
        result = result * jnp.where((size >> i) & 1 == 1, factor, np.float32(1.0))
    return result


def exponent_of(value):
    largest = jnp.max(jnp.abs(value), axis=(0, 1), keepdims=True)
    return jnp.ceil(jnp.log(jnp.maximum(largest, 1e-30)) * np.float32(1.4426950408889634)).astype(jnp.int32)


def rows_of(comps):
    return -(-S * len(comps) // 8) * 8


def cross_kernel(comps, ids_ref, src_block_ref, owner_ref, recv_ref, signs_ref, *rest):
    blocks, (o_ref, src) = rest[:-2], rest[-2:]
    rows = rows_of(comps)
    columns = recv_ref.shape[1]
    half = recv_ref.shape[2] // 2
    for k in range(S // SB):
        which = ids_ref[1] ^ src_block_ref[k]
        for j in range(len(blocks)):

            @pl.when(which == j)
            def _():
                for station in range(SB):
                    mask = ids_ref[0] ^ owner_ref[k * SB + station]
                    for a in range(len(comps)):
                        src[mask * len(comps) + a, 0:F] = blocks[j][a, station].astype(f32)

    flat = src.reshape(rows * XF, src.shape[2])
    signs = signs_ref[...]

    def one_freq(f, carry):
        plain = flat[pl.ds(f, rows, stride=XF), :]
        rolled = pltpu.roll(plain, half, 1)
        left = [plain * signs[0:1], plain * signs[1:2], rolled * signs[2:3], rolled * signs[3:4]]
        left = jnp.concatenate(left, axis=0).astype(bf16)
        out = lax.dot_general(left, recv_ref[f], (((1,), (1,)), ((), ())), preferred_element_type=f32)
        o_ref[pl.ds(f, G * rows, stride=XS), 0:columns] = out[: G * rows]
        o_ref[pl.ds(F + f, G * rows, stride=XS), 0:columns] = out[G * rows :]
        return carry

    lax.fori_loop(0, F, one_freq, 0, unroll=F)


def cross_spectra(comps, ids, src_block, owner, recv, signs, blocks):
    depth = recv.shape[2]
    rows = rows_of(comps)
    return pl.pallas_call(
        functools.partial(cross_kernel, comps),
        in_specs=[SMEM] * 3 + [VMEM] * (2 + len(blocks)),
        out_specs=VMEM,
        out_shape=jax.ShapeDtypeStruct((G * rows * XS, 128), f32),
        scratch_shapes=[pltpu.VMEM((rows, XF, depth), f32)],
        compiler_params=PARAMS,
        cost_estimate=pl.CostEstimate(flops=0, bytes_accessed=10 << 20, transcendentals=0),
        name="cross_spectra",
    )(ids, src_block, owner, recv, signs, *blocks)


def lag_kernel(outputs, held, columns, cross_ref, table_ref, scale_ref, *o_refs):
    rows = rows_of(held)
    table_high, table_low = two_terms(table_ref[...])
    table = jnp.concatenate([table_high, table_low], axis=1)
    for (coded, blocks_of), o_ref in zip(outputs, o_refs):
        exponents = jnp.zeros((TAIL, LAG), f32)
        done = 0
        for at, (mask, comps) in enumerate(blocks_of):
            turned = []
            for g in range(G):
                for a in comps:
                    first = (g * rows + mask * len(held) + held.index(a)) * XS
                    turned.append(cross_ref[first : first + 2 * F, :].T[:columns])
            high, low = two_terms(jnp.concatenate(turned, axis=0))
            both = jnp.dot(high, table, preferred_element_type=f32)
            lagged = both[:, :LAG] + both[:, LAG:] + jnp.dot(low, table_high, preferred_element_type=f32)
            part = len(comps) * columns
            lagged = [lagged[g * part : (g + 1) * part] * scale_ref[g : g + 1] for g in range(G)]
            lagged = jnp.concatenate(lagged, axis=0)
            if coded:
                e = exponent_of(lagged)
                lagged = lagged * power_of_two(TOP - e)
                exponents = jnp.where(lax.broadcasted_iota(jnp.int32, (TAIL, LAG), 0) == at, e.astype(f32), exponents)
            o_ref[done : done + G * part] = lagged
            done += G * part
        if coded:
            o_ref[done:] = exponents


def lag_transform(outputs, held, columns, cross, table, scale):
    shapes = []
    for coded, blocks_of in outputs:
        size = sum(G * len(comps) * columns for _, comps in blocks_of) + (TAIL if coded else 0)
        shapes.append(jax.ShapeDtypeStruct((size, LAG), f32))
    return pl.pallas_call(
        functools.partial(lag_kernel, outputs, held, columns),
        in_specs=[VMEM] * 3,
        out_specs=[VMEM] * len(outputs),
        out_shape=shapes,
        compiler_params=PARAMS,
        cost_estimate=pl.CostEstimate(flops=0, bytes_accessed=5 << 20, transcendentals=0),
        name="lag_transform",
    )(cross, table, scale)


def factor_of(coded_ref, at):
    return power_of_two(coded_ref[at : at + 1, 0:1].astype(jnp.int32) - TOP)


def merge_kernel(counts, outputs, *refs):
    sums, o_refs = refs[: 2 * len(counts)], refs[2 * len(counts) :]
    for (coded, blocks_of), o_ref in zip(outputs, o_refs):
        exponents = jnp.zeros((TAIL, LAG), f32)
        done = 0
        for at, (i, j) in enumerate(blocks_of):
            kept_ref, arrived_ref = sums[2 * i : 2 * i + 2]
            size = (kept_ref.shape[0] - TAIL) // counts[i]
            rows = slice(j * size, (j + 1) * size)
            here, there = [ref[counts[i] * size + j : counts[i] * size + j + 1, 0:1].astype(jnp.int32) for ref in (kept_ref, arrived_ref)]
            e = jnp.maximum(here, there) + 1 if coded else jnp.full((1, 1), TOP, jnp.int32)
            value = kept_ref[rows] * power_of_two(here - e) + arrived_ref[rows] * power_of_two(there - e)
            if coded:
                exponents = jnp.where(lax.broadcasted_iota(jnp.int32, (TAIL, LAG), 0) == at, e.astype(f32), exponents)
            o_ref[done : done + size] = value
            done += size
        if coded:
            o_ref[done:] = exponents


def merge(sums, outputs):
    shapes = []
    for coded, blocks_of in outputs:
        size = sum((sums[i][1].shape[0] - TAIL) // sums[i][0] for i, _ in blocks_of) + (TAIL if coded else 0)
        shapes.append(jax.ShapeDtypeStruct((size, LAG), f32))
    return pl.pallas_call(
        functools.partial(merge_kernel, [count for count, _, _ in sums], outputs),
        in_specs=[VMEM] * (2 * len(sums)),
        out_specs=[VMEM] * len(outputs),
        out_shape=shapes,
        compiler_params=PARAMS,
        name="merge",
    )(*[array for _, *arrays in sums for array in arrays])


def total_kernel(stations, terms, *refs):
    refs, o_ref = refs[:-1], refs[-1]
    per_station = G * COMPS * COMPS
    for comps, parts in terms:
        factors = [None if at is None else factor_of(refs[i], at) for i, _, at in parts]
        done = 0
        for g in range(G):
            for a in comps:
                for b in range(COMPS):
                    value = None
                    for (i, first, _), factor in zip(parts, factors):
                        part = refs[i][first + done : first + done + stations, :]
                        part = part if factor is None else part * factor
                        value = part if value is None else value + part
                    done += stations
                    o_ref[pl.ds((a * COMPS + b) * G + g, stations, stride=per_station), :] = value


def total(stations, terms, arrays):
    return pl.pallas_call(
        functools.partial(total_kernel, stations, terms),
        in_specs=[VMEM] * len(arrays),
        out_specs=VMEM,
        out_shape=jax.ShapeDtypeStruct((stations * COMPS * COMPS * G, LAG), f32),
        compiler_params=PARAMS,
        name="total",
    )(*arrays)


def swap(value, axis, mask):
    size = lax.axis_size(axis)
    return lax.ppermute(value, axis, [(i, i ^ mask) for i in range(size)])


def send(coded, mask):
    return swap(coded.astype(f16), "day", mask).astype(f32)


def owned_block(owner):
    ids = jnp.arange(owner.shape[0], dtype=jnp.int32)
    return jnp.sum(ids[None, :] * (owner[None, :] == ids[:, None]).astype(jnp.int32), axis=1)


def local(spectra, src_block, group_of, owner):
    stations = spectra.shape[3]
    days = lax.axis_size("day")
    ids = jnp.stack([lax.axis_index("day"), lax.axis_index("sta")])
    recv, signs, scale = receivers_by_freq(ids, spectra, group_of)
    columns = COMPS * stations
    table = jnp.asarray(lag_table(F, LAG))
    block_rows = S * stations // days

    if days == S and lax.axis_size("sta") == 4:
        ahead, rest = (2,), (0, 1)
        near, far = [0, 2], [6, 4]
        early, late = first_block(spectra, (ahead, rest))
        across = swap(early, "sta", 2)
        beside, late = lax.optimization_barrier((swap(early, "sta", 1), late))
        across_late = swap(late, "sta", 2)
        across, recv, signs, scale, table = lax.optimization_barrier((across, recv, signs, scale, table))
        early = [early, beside, across, swap(across, "sta", 1)]
        cross = cross_spectra(ahead, ids, src_block, owner, recv, signs, early)
        away, kept = lag_transform(
            [(True, [(1 ^ z, ahead) for z in near + far]), (True, [(z, ahead) for z in near + far])],
            ahead,
            columns,
            cross,
            table,
            scale,
        )
        across_late, away, kept = lax.optimization_barrier((across_late, away, kept))
        arrived = send(away, 1)
        late = [late, swap(late, "sta", 1), across_late, swap(across_late, "sta", 1)]
        cross = cross_spectra(rest, ids, src_block, owner, recv, signs, late)
        lags = functools.partial(lag_transform, held=rest, columns=columns, cross=cross, table=table, scale=scale)
        (away_far,) = lags([(True, [(1 ^ z, rest) for z in far])])
        away_far, cross = lax.optimization_barrier((away_far, cross))
        arrived_far = send(away_far, 1)
        (away_near,) = lags([(True, [(2, rest), (3, rest)])], cross=cross)
        arrived_near = send(away_near, 2)
        kept, away = merge([(4, kept, arrived)], [(True, [(0, 0), (0, 1)]), (True, [(0, 3), (0, 2)])])
        arrived = send(away, 4)
        kept_near, kept_far = lags([(True, [(z, rest) for z in of]) for of in ((0, 1), far)], cross=cross)
        by_6, by_4 = merge([(2, kept_far, arrived_far)], [(True, [(0, 0)]), (True, [(0, 1)])])
        kept_near, by_6, by_4 = lax.optimization_barrier((kept_near, by_6, by_4))
        by_6 = send(by_6, 6)
        by_4 = send(by_4, 4)
        own_rest, by_1 = merge([(2, kept_near, arrived_near)], [(False, [(0, 0)]), (True, [(0, 1)])])
        by_1 = send(by_1, 1)
        own_ahead, ahead_by_2 = merge([(2, kept, arrived)], [(False, [(0, 0)]), (True, [(0, 1)])])
        ahead_by_2 = send(ahead_by_2, 2)
        size, ahead_size = own_rest.shape[0], own_ahead.shape[0]
        terms = [
            (rest, [(0, 0, None), (1, 0, size), (2, 0, size), (3, 0, size)]),
            (ahead, [(4, 0, None), (5, 0, ahead_size)]),
        ]
        result = total(stations, terms, [own_rest, by_1, by_6, by_4, own_ahead, ahead_by_2])
        result = result.reshape(block_rows, COMPS * COMPS, G, LAG).transpose(0, 2, 1, 3)
        return result[None]

    every = tuple(range(COMPS))
    (first,) = first_block(spectra, (every,))
    gathered = lax.all_gather(first, "sta")
    blocks = [lax.dynamic_index_in_dim(gathered, src_block[k], 0, keepdims=False) for k in range(2)]
    order = jnp.arange(S, dtype=jnp.int32)
    cross = cross_spectra(every, jnp.zeros(2, jnp.int32), order[:2], order, recv, signs, blocks)
    outputs = [(False, [(mask, every) for mask in range(S)])]
    (partial,) = lag_transform(outputs, every, columns, cross, table, scale)
    partial = partial.reshape(S, G, COMPS * COMPS, stations, LAG).transpose(0, 3, 1, 2, 4)
    partial = partial.reshape(days, block_rows, G, COMPS * COMPS, LAG)
    ordered = jnp.take(partial, owned_block(owner), axis=0)
    return lax.psum_scatter(ordered, "day", scatter_dimension=0, tiled=True)


def solution(mesh):
    return jax.shard_map(
        local,
        mesh=mesh,
        in_specs=(P("day", None, None, "sta", None), P(), P(), P()),
        out_specs=P("day", "sta", None, None, None),
        check_vma=False,
    )
```

```python
import functools

import jax
import jax.numpy as jnp
import numpy as np
from jax import lax
from jax.experimental import pallas as pl
from jax.experimental.pallas import tpu as pltpu
from jax.sharding import PartitionSpec as P

F = 128
LAG = 128
G = 2
SB = 4
S = 8
COMPS = 3
XF = F + 8
XS = 2 * F + 8

f32 = jnp.float32
bf16 = jnp.bfloat16
f16 = jnp.float16
TAIL = 8
TOP = 14
PARAMS = pltpu.CompilerParams(vmem_limit_bytes=24 << 20)
VMEM = pl.BlockSpec(memory_space=pltpu.VMEM)
SMEM = pl.BlockSpec(memory_space=pltpu.SMEM)


def lag_table(freqs, lags):
    freq_ids = np.arange(freqs)
    lag_ids = np.arange(lags) - lags // 2
    angle = 2.0 * np.pi / (2 * freqs) * np.mod(freq_ids[:, None] * lag_ids[None, :], 2 * freqs)
    weight = np.where(freq_ids == 0, 1.0, 2.0)[:, None] / np.sqrt(freqs)
    return np.concatenate([weight * np.cos(angle), -weight * np.sin(angle)], axis=0).astype(np.float32)


def two_terms(value):
    high = value.astype(bf16)
    return high, (value - high.astype(f32)).astype(bf16)


def first_kernel(shares, x_ref, *refs):
    o_refs, wide = refs[:-1], refs[-1]
    rows = x_ref.shape[0] * 2
    for a in range(COMPS):
        for part in range(2):
            wide[a, part] = x_ref[:, part, a, 0:8].astype(f32)
        flat = wide.at[a].reshape(rows * 8, F)
        for of, o_ref in zip(shares, o_refs):
            if a in of:
                for s in range(SB):
                    o_ref[of.index(a), s] = flat[pl.ds(s, rows, stride=8), :].T.astype(bf16)


def first_block(spectra, shares):
    segs = spectra.shape[0]
    return pl.pallas_call(
        functools.partial(first_kernel, shares),
        in_specs=[VMEM],
        out_specs=[VMEM] * len(shares),
        out_shape=[jax.ShapeDtypeStruct((len(of), SB, F, 2 * segs), bf16) for of in shares],
        scratch_shapes=[pltpu.VMEM((COMPS, 2, segs, 8, F), f32)],
        compiler_params=PARAMS,
        name="first_block",
    )(spectra)


def receivers_kernel(ids_ref, x_ref, group_ref, o_ref, signs_ref, scale_ref, wide, turned):
    rows = x_ref.shape[0] * 2
    stations = x_ref.shape[3]
    columns = COMPS * stations
    at = ids_ref[0] * (rows // 2)
    row = group_ref[pl.ds(at // rows, 1), :].astype(f32)
    swapped = pltpu.roll(row, rows // 2, 1)
    low = lax.broadcasted_iota(jnp.int32, row.shape, 1) < rows // 2
    mine = jnp.where(low == (at % rows == 0), row, swapped)
    for g in range(G):
        hot = jnp.where(mine == g, np.float32(1.0), np.float32(0.0))
        signs_ref[g : g + 1] = hot
        signs_ref[G + g : G + g + 1] = jnp.where(low, -hot, hot)
        hits = jnp.where(group_ref[...] == g, np.float32(1.0), np.float32(0.0))
        count = jnp.sum(hits, axis=(0, 1), keepdims=True)
        scale_ref[g : g + 1] = jnp.broadcast_to(1.0 / jnp.sqrt(count), (1, LAG))
    for b in range(COMPS):
        for part in range(2):
            wide[b, part] = x_ref[:, part, b].astype(f32)
        flat = wide.at[b].reshape(rows * stations, F)
        for r in range(stations):
            turned[pl.ds(b * stations + r, F, stride=columns), :] = flat[pl.ds(r, rows, stride=stations), :].T

    def body(f, carry):
        o_ref[f] = turned[pl.ds(pl.multiple_of(f * columns, 8), columns), :].astype(bf16)
        return carry

    lax.fori_loop(0, F, body, 0, unroll=16)


def receivers_by_freq(ids, spectra, group_of):
    segs, stations = spectra.shape[0], spectra.shape[3]
    columns = COMPS * stations
    groups = group_of.reshape(-1, 2 * segs)
    return pl.pallas_call(
        receivers_kernel,
        in_specs=[SMEM, VMEM, VMEM],
        out_specs=[VMEM] * 3,
        out_shape=[
            jax.ShapeDtypeStruct((F, columns, 2 * segs), bf16),
            jax.ShapeDtypeStruct((2 * G, 2 * segs), f32),
            jax.ShapeDtypeStruct((G, LAG), f32),
        ],
        scratch_shapes=[pltpu.VMEM((COMPS, 2, segs, stations, F), f32), pltpu.VMEM((F * columns, 2 * segs), f32)],
        compiler_params=PARAMS,
        cost_estimate=pl.CostEstimate(flops=0, bytes_accessed=12 << 20, transcendentals=0),
        name="receivers_by_freq",
    )(ids, spectra, groups)


def power_of_two(n):
    size = jnp.abs(n)
    result = jnp.ones(n.shape, f32)
    for i in range(7):
        factor = jnp.where(n < 0, np.float32(2.0 ** -(2**i)), np.float32(2.0 ** (2**i)))
        result = result * jnp.where((size >> i) & 1 == 1, factor, np.float32(1.0))
    return result


def exponent_of(value):
    largest = jnp.max(jnp.abs(value), axis=(0, 1), keepdims=True)
    return jnp.ceil(jnp.log(jnp.maximum(largest, 1e-30)) * np.float32(1.4426950408889634)).astype(jnp.int32)


def rows_of(comps):
    return -(-S * len(comps) // 8) * 8


def cross_kernel(comps, ids_ref, src_block_ref, owner_ref, recv_ref, signs_ref, *rest):
    blocks, (o_ref, src) = rest[:-2], rest[-2:]
    rows = rows_of(comps)
    columns = recv_ref.shape[1]
    half = recv_ref.shape[2] // 2
    for k in range(S // SB):
        which = ids_ref[1] ^ src_block_ref[k]
        for j in range(len(blocks)):

            @pl.when(which == j)
            def _():
                for station in range(SB):
                    mask = ids_ref[0] ^ owner_ref[k * SB + station]
                    for a in range(len(comps)):
                        src[mask * len(comps) + a, 0:F] = blocks[j][a, station].astype(f32)

    flat = src.reshape(rows * XF, src.shape[2])
    signs = signs_ref[...]

    def one_freq(f, carry):
        plain = flat[pl.ds(f, rows, stride=XF), :]
        rolled = pltpu.roll(plain, half, 1)
        left = [plain * signs[0:1], plain * signs[1:2], rolled * signs[2:3], rolled * signs[3:4]]
        left = jnp.concatenate(left, axis=0).astype(bf16)
        out = lax.dot_general(left, recv_ref[f], (((1,), (1,)), ((), ())), preferred_element_type=f32)
        o_ref[pl.ds(f, G * rows, stride=XS), 0:columns] = out[: G * rows]
        o_ref[pl.ds(F + f, G * rows, stride=XS), 0:columns] = out[G * rows :]
        return carry

    lax.fori_loop(0, F, one_freq, 0, unroll=F)


def cross_spectra(comps, ids, src_block, owner, recv, signs, blocks):
    depth = recv.shape[2]
    rows = rows_of(comps)
    return pl.pallas_call(
        functools.partial(cross_kernel, comps),
        in_specs=[SMEM] * 3 + [VMEM] * (2 + len(blocks)),
        out_specs=VMEM,
        out_shape=jax.ShapeDtypeStruct((G * rows * XS, 128), f32),
        scratch_shapes=[pltpu.VMEM((rows, XF, depth), f32)],
        compiler_params=PARAMS,
        cost_estimate=pl.CostEstimate(flops=0, bytes_accessed=10 << 20, transcendentals=0),
        name="cross_spectra",
    )(ids, src_block, owner, recv, signs, *blocks)


def lag_kernel(outputs, held, columns, cross_ref, table_ref, scale_ref, *o_refs):
    rows = rows_of(held)
    table_high, table_low = two_terms(table_ref[...])
    table = jnp.concatenate([table_high, table_low], axis=1)
    for (coded, blocks_of), o_ref in zip(outputs, o_refs):
        exponents = jnp.zeros((TAIL, LAG), f32)
        done = 0
        for at, (mask, comps) in enumerate(blocks_of):
            turned = []
            for g in range(G):
                for a in comps:
                    first = (g * rows + mask * len(held) + held.index(a)) * XS
                    turned.append(cross_ref[first : first + 2 * F, :].T[:columns])
            high, low = two_terms(jnp.concatenate(turned, axis=0))
            both = jnp.dot(high, table, preferred_element_type=f32)
            lagged = both[:, :LAG] + both[:, LAG:] + jnp.dot(low, table_high, preferred_element_type=f32)
            part = len(comps) * columns
            lagged = [lagged[g * part : (g + 1) * part] * scale_ref[g : g + 1] for g in range(G)]
            lagged = jnp.concatenate(lagged, axis=0)
            if coded:
                e = exponent_of(lagged)
                lagged = lagged * power_of_two(TOP - e)
                exponents = jnp.where(lax.broadcasted_iota(jnp.int32, (TAIL, LAG), 0) == at, e.astype(f32), exponents)
            o_ref[done : done + G * part] = lagged
            done += G * part
        if coded:
            o_ref[done:] = exponents


def lag_transform(outputs, held, columns, cross, table, scale):
    shapes = []
    for coded, blocks_of in outputs:
        size = sum(G * len(comps) * columns for _, comps in blocks_of) + (TAIL if coded else 0)
        shapes.append(jax.ShapeDtypeStruct((size, LAG), f32))
    return pl.pallas_call(
        functools.partial(lag_kernel, outputs, held, columns),
        in_specs=[VMEM] * 3,
        out_specs=[VMEM] * len(outputs),
        out_shape=shapes,
        compiler_params=PARAMS,
        cost_estimate=pl.CostEstimate(flops=0, bytes_accessed=5 << 20, transcendentals=0),
        name="lag_transform",
    )(cross, table, scale)


def factor_of(coded_ref, at):
    return power_of_two(coded_ref[at : at + 1, 0:1].astype(jnp.int32) - TOP)


def merge_kernel(counts, outputs, *refs):
    sums, o_refs = refs[: 2 * len(counts)], refs[2 * len(counts) :]
    for (coded, blocks_of), o_ref in zip(outputs, o_refs):
        exponents = jnp.zeros((TAIL, LAG), f32)
        done = 0
        for at, (i, j) in enumerate(blocks_of):
            kept_ref, arrived_ref = sums[2 * i : 2 * i + 2]
            size = (kept_ref.shape[0] - TAIL) // counts[i]
            rows = slice(j * size, (j + 1) * size)
            here, there = [ref[counts[i] * size + j : counts[i] * size + j + 1, 0:1].astype(jnp.int32) for ref in (kept_ref, arrived_ref)]
            e = jnp.maximum(here, there) + 1 if coded else jnp.full((1, 1), TOP, jnp.int32)
            value = kept_ref[rows] * power_of_two(here - e) + arrived_ref[rows] * power_of_two(there - e)
            if coded:
                exponents = jnp.where(lax.broadcasted_iota(jnp.int32, (TAIL, LAG), 0) == at, e.astype(f32), exponents)
            o_ref[done : done + size] = value
            done += size
        if coded:
            o_ref[done:] = exponents


def merge(sums, outputs):
    shapes = []
    for coded, blocks_of in outputs:
        size = sum((sums[i][1].shape[0] - TAIL) // sums[i][0] for i, _ in blocks_of) + (TAIL if coded else 0)
        shapes.append(jax.ShapeDtypeStruct((size, LAG), f32))
    return pl.pallas_call(
        functools.partial(merge_kernel, [count for count, _, _ in sums], outputs),
        in_specs=[VMEM] * (2 * len(sums)),
        out_specs=[VMEM] * len(outputs),
        out_shape=shapes,
        compiler_params=PARAMS,
        name="merge",
    )(*[array for _, *arrays in sums for array in arrays])


def total_kernel(stations, terms, *refs):
    refs, o_ref = refs[:-1], refs[-1]
    per_station = G * COMPS * COMPS
    for comps, parts in terms:
        factors = [None if at is None else factor_of(refs[i], at) for i, _, at in parts]
        done = 0
        for g in range(G):
            for a in comps:
                for b in range(COMPS):
                    value = None
                    for (i, first, _), factor in zip(parts, factors):
                        part = refs[i][first + done : first + done + stations, :]
                        part = part if factor is None else part * factor
                        value = part if value is None else value + part
                    done += stations
                    o_ref[pl.ds((a * COMPS + b) * G + g, stations, stride=per_station), :] = value


def total(stations, terms, arrays):
    return pl.pallas_call(
        functools.partial(total_kernel, stations, terms),
        in_specs=[VMEM] * len(arrays),
        out_specs=VMEM,
        out_shape=jax.ShapeDtypeStruct((stations * COMPS * COMPS * G, LAG), f32),
        compiler_params=PARAMS,
        name="total",
    )(*arrays)


def swap(value, axis, mask):
    size = lax.axis_size(axis)
    return lax.ppermute(value, axis, [(i, i ^ mask) for i in range(size)])


def send(coded, mask):
    return swap(coded.astype(f16), "day", mask).astype(f32)


def owned_block(owner):
    ids = jnp.arange(owner.shape[0], dtype=jnp.int32)
    return jnp.sum(ids[None, :] * (owner[None, :] == ids[:, None]).astype(jnp.int32), axis=1)


def local(spectra, src_block, group_of, owner):
    stations = spectra.shape[3]
    days = lax.axis_size("day")
    ids = jnp.stack([lax.axis_index("day"), lax.axis_index("sta")])
    recv, signs, scale = receivers_by_freq(ids, spectra, group_of)
    columns = COMPS * stations
    table = jnp.asarray(lag_table(F, LAG))
    block_rows = S * stations // days

    if days == S and lax.axis_size("sta") == 4:
        ahead, rest = (2,), (0, 1)
        near, far = [0, 2], [6, 4]
        early, late = first_block(spectra, (ahead, rest))
        across = swap(early, "sta", 2)
        beside, late = lax.optimization_barrier((swap(early, "sta", 1), late))
        across_late = swap(late, "sta", 2)
        across, recv, signs, scale, table = lax.optimization_barrier((across, recv, signs, scale, table))
        early = [early, beside, across, swap(across, "sta", 1)]
        cross = cross_spectra(ahead, ids, src_block, owner, recv, signs, early)
        away, kept = lag_transform(
            [(True, [(1 ^ z, ahead) for z in near + far]), (True, [(z, ahead) for z in near + far])],
            ahead,
            columns,
            cross,
            table,
            scale,
        )
        across_late, away, kept = lax.optimization_barrier((across_late, away, kept))
        arrived = send(away, 1)
        late = [late, swap(late, "sta", 1), across_late, swap(across_late, "sta", 1)]
        cross = cross_spectra(rest, ids, src_block, owner, recv, signs, late)
        lags = functools.partial(lag_transform, held=rest, columns=columns, cross=cross, table=table, scale=scale)
        (away_far,) = lags([(True, [(1 ^ z, rest) for z in far])])
        away_far, cross = lax.optimization_barrier((away_far, cross))
        arrived_far = send(away_far, 1)
        (away_near,) = lags([(True, [(2, rest), (3, rest)])], cross=cross)
        arrived_near = send(away_near, 2)
        kept, away = merge([(4, kept, arrived)], [(True, [(0, 0), (0, 1)]), (True, [(0, 3), (0, 2)])])
        arrived = send(away, 4)
        kept_near, kept_far = lags([(True, [(z, rest) for z in of]) for of in ((0, 1), far)], cross=cross)
        by_6, by_4 = merge([(2, kept_far, arrived_far)], [(True, [(0, 0)]), (True, [(0, 1)])])
        kept_near, by_6, by_4 = lax.optimization_barrier((kept_near, by_6, by_4))
        by_6 = send(by_6, 6)
        by_4 = send(by_4, 4)
        own_rest, by_1 = merge([(2, kept_near, arrived_near)], [(False, [(0, 0)]), (True, [(0, 1)])])
        by_1 = send(by_1, 1)
        own_ahead, ahead_by_2 = merge([(2, kept, arrived)], [(False, [(0, 0)]), (True, [(0, 1)])])
        ahead_by_2 = send(ahead_by_2, 2)
        size, ahead_size = own_rest.shape[0], own_ahead.shape[0]
        terms = [
            (rest, [(0, 0, None), (1, 0, size), (2, 0, size), (3, 0, size)]),
            (ahead, [(4, 0, None), (5, 0, ahead_size)]),
        ]
        result = total(stations, terms, [own_rest, by_1, by_6, by_4, own_ahead, ahead_by_2])
        result = result.reshape(block_rows, COMPS * COMPS, G, LAG).transpose(0, 2, 1, 3)
        return result[None]

    every = tuple(range(COMPS))
    (first,) = first_block(spectra, (every,))
    gathered = lax.all_gather(first, "sta")
    blocks = [lax.dynamic_index_in_dim(gathered, src_block[k], 0, keepdims=False) for k in range(2)]
    order = jnp.arange(S, dtype=jnp.int32)
    cross = cross_spectra(every, jnp.zeros(2, jnp.int32), order[:2], order, recv, signs, blocks)
    outputs = [(False, [(mask, every) for mask in range(S)])]
    (partial,) = lag_transform(outputs, every, columns, cross, table, scale)
    partial = partial.reshape(S, G, COMPS * COMPS, stations, LAG).transpose(0, 3, 1, 2, 4)
    partial = partial.reshape(days, block_rows, G, COMPS * COMPS, LAG)
    ordered = jnp.take(partial, owned_block(owner), axis=0)
    return lax.psum_scatter(ordered, "day", scatter_dimension=0, tiled=True)


def solution(mesh):
    return jax.shard_map(
        local,
        mesh=mesh,
        in_specs=(P("day", None, None, "sta", None), P(), P(), P()),
        out_specs=P("day", "sta", None, None, None),
        check_vma=False,
    )
```
